512 devices in a mesh: ctx: 64 (over z_lo, y, core), tp: 8 (over x, z_hi).
Axes of the slice: x: 4, y: 4, z: 16 (z_hi: 2, z_lo: 8; z = z_hi * 8 + z_lo), core: 2. Of those that a mesh axis runs over, the one named last changes fastest.
Arguments:
- queries: bfloat16 [4, 64, 8192], P(None, 'ctx', 'tp'), may hold values from -15 to 15
- cache_keys: bfloat16 [4, 131072, 1024], P(None, 'ctx', 'tp'), may hold values from -6 to 6
- cache_values: bfloat16 [4, 131072, 1024], P(None, 'ctx', 'tp'), may hold values from -6 to 6
- new_keys: bfloat16 [4, 64, 1024], P(None, 'ctx', 'tp'), may hold values from -6 to 6
- new_values: bfloat16 [4, 64, 1024], P(None, 'ctx', 'tp'), may hold values from -6 to 6
- out_weight: bfloat16 [8192, 8192], P('tp', 'ctx'), may hold values from -0.0625 to 0.0625
Outputs:
- projected: bfloat16 [4, 64, 8192], P(None, 'tp', 'ctx')
The draws below stay inside these ranges and needn't reach their ends.
All inputs are finite; a program needn't handle non-finite values.
Results may differ from the reference program's by a relative error of at most 0.017.
Values may be sent and summed in bfloat16 or wider, within the bound.
A program may use at most 192 MiB of HBM per device.

```python
import math
import jax
import jax.numpy as jnp
from jax import lax

D = 8192
HEADS = 64
KVH = 8
HD = 128
NEW = 64
SEQS = 4
CTX_DEV = 2048
CTX = 131072
QW = 8192
KW = 1024
N_CTX = 64


def draw_queries(key, part):
    key = jax.random.fold_in(key, 3)
    draw_shape = (SEQS, NEW, HEADS * HD)
    values_out = jnp.clip(3.0 * jax.random.normal(key, draw_shape, jnp.float32), -15.0, 15.0)
    return values_out.astype(jnp.bfloat16)


def draw_cache_keys(key, part):
    key = jax.random.fold_in(key, 5)
    draw_shape = (SEQS, CTX, KVH * HD)
    values_out = jnp.clip(jax.random.normal(key, draw_shape, jnp.float32), -6.0, 6.0)
    return values_out.astype(jnp.bfloat16)


def levels(stream_key, shape, cuts, least, largest):
    gain = 1.0
    for position, parts in cuts:
        draws = jax.random.uniform(jax.random.fold_in(jax.random.fold_in(stream_key, 6), position), (parts,), jnp.float32, least / len(cuts), largest / len(cuts))
        gain = gain * jnp.repeat(jnp.exp(draws), shape[position] // parts).reshape((-1,) + (1,) * (len(shape) - 1 - position))
    return gain


def centred(rng, shape, spread, bound, shards=(), kind=jnp.bfloat16):
    loudness = levels(rng, shape, shards, -0.22, 0.18) if shards else 1.0
    result = jax.random.normal(rng, shape, jnp.float32) * spread * loudness
    return jnp.minimum(jnp.maximum(result, -bound), bound).astype(kind)


def setup_inputs(seed: int = 0) -> dict:
    key_of = jax.random.split(jax.random.key(seed), 7)
    queries = draw_queries(jax.random.fold_in(key_of[6], 71), 0)
    cache_keys = draw_cache_keys(jax.random.fold_in(key_of[6], 71), 0)
    cache_values = centred(key_of[2], (SEQS, CTX, KW), 1.0, 6.0, ((1, 64), (2, 8)))
    new_keys = centred(key_of[3], (SEQS, NEW, KW), 1.0, 6.0, ((1, 64), (2, 8)))
    new_values = centred(key_of[4], (SEQS, NEW, KW), 1.0, 6.0, ((1, 64), (2, 8)))
    out_weight = centred(key_of[5], (QW, D), QW ** -0.5, 0.0625, ((0, 8), (1, 64)))
    return {"queries": queries, "cache_keys": cache_keys, "cache_values": cache_values, "new_keys": new_keys, "new_values": new_values, "out_weight": out_weight}


def slab_terms(query_heads, key_block, value_block, new_key_block, new_value_block, visible):
    inv_root = 1.0 / math.sqrt(HD)
    scores = jnp.einsum('tkgd,skd->tkgs', query_heads, key_block.astype(jnp.float32)) * inv_root
    fresh_scores = jnp.einsum('tkgd,skd->tkgs', query_heads, new_key_block.astype(jnp.float32)) * inv_root
    fresh_scores = jnp.where(visible[:, None, None, :], fresh_scores, -jnp.inf)
    row_peak = jnp.maximum(lax.optimization_barrier(jnp.max(scores, axis=-1)), lax.optimization_barrier(jnp.max(fresh_scores, axis=-1)))
    old_weights = jnp.exp(scores - row_peak[..., None])
    new_weights = jnp.exp(fresh_scores - row_peak[..., None])
    weight_sum = lax.optimization_barrier(jnp.sum(old_weights, axis=-1)) + lax.optimization_barrier(jnp.sum(new_weights, axis=-1))
    rounded_old = lax.optimization_barrier(old_weights.astype(jnp.bfloat16)).astype(jnp.float32)
    rounded_new = lax.optimization_barrier(new_weights.astype(jnp.bfloat16)).astype(jnp.float32)
    numerator = jnp.einsum('tkgs,skd->tkgd', rounded_old, value_block.astype(jnp.float32))
    numerator = numerator + jnp.einsum('tkgs,skd->tkgd', rounded_new, new_value_block.astype(jnp.float32))
    return (row_peak, weight_sum, numerator)

def reference(queries, cache_keys, cache_values, new_keys, new_values, out_weight):
    per_group = HEADS // KVH
    own_new = NEW // N_CTX
    token_pos = jnp.arange(NEW, dtype=jnp.int32)

    def attend_one(inputs_one):
        query_one, keys_one, values_one, newk_one, newv_one = inputs_one
        query_heads = query_one.astype(jnp.float32).reshape(NEW, KVH, per_group, HD)
        key_slabs = keys_one.reshape(N_CTX, CTX_DEV, KVH, HD)
        value_slabs = values_one.reshape(N_CTX, CTX_DEV, KVH, HD)
        newk_slabs = newk_one.reshape(N_CTX, own_new, KVH, HD)
        newv_slabs = newv_one.reshape(N_CTX, own_new, KVH, HD)

        def slab_step(carry, slab_in):
            key_block, value_block, newk_block, newv_block, slab_index = slab_in
            key_pos = slab_index * own_new + jnp.arange(own_new, dtype=jnp.int32)
            visible = key_pos[None, :] <= token_pos[:, None]
            return (carry, slab_terms(query_heads, key_block, value_block, newk_block, newv_block, visible))
        _, (peaks, sums, numers) = lax.scan(slab_step, jnp.zeros((), jnp.float32), (key_slabs, value_slabs, newk_slabs, newv_slabs, jnp.arange(N_CTX, dtype=jnp.int32)))
        global_peak = lax.optimization_barrier(jnp.max(peaks, axis=0))
        factor = jnp.exp(peaks - global_peak[None])
        total = lax.optimization_barrier(jnp.sum(sums * factor, axis=0))
        numer = lax.optimization_barrier(jnp.sum(numers * factor[..., None], axis=0))
        return (numer / total[..., None]).reshape(NEW, HEADS * HD).astype(jnp.bfloat16)
    attended = lax.map(attend_one, (queries, cache_keys, cache_values, new_keys, new_values))
    projected = jnp.einsum('snq,qd->snd', attended.astype(jnp.float32), out_weight.astype(jnp.float32))
    return projected.astype(jnp.bfloat16)
```

```python
import functools
import math

import jax
import jax.numpy as jnp
from jax import lax
from jax.experimental import pallas as pl
from jax.experimental.pallas import tpu as pltpu
from jax.sharding import PartitionSpec as P

HD = 128
HEADS = 8
SEQS = 4
UNIT = SEQS * HEADS
PAD = 16
CHUNK = 256
SCALE = math.log2(math.e) / math.sqrt(HD)
MESH = pl.DeviceIdType.MESH
F32 = jnp.float32
BF16 = jnp.bfloat16


def iota(shape, dim):
    return lax.broadcasted_iota(jnp.int32, shape, dim)


def loop(first, last, body):
    lax.fori_loop(first, last, lambda i, c: (body(i), c)[1], 0)


def rounded(x):
    return x.astype(BF16).astype(F32)


def spread(packed, first):
    shape = (packed.shape[0], UNIT, HD)
    wide = jnp.broadcast_to(packed[:, None, :], shape)
    hit = iota(shape, 2) == iota(shape, 1) + first
    return jnp.sum(jnp.where(hit, wide, 0.0), axis=-1, keepdims=True)


def merge(stats, numers):
    peak = functools.reduce(jnp.maximum, stats)
    factors = [jnp.exp2(s - peak) for s in stats]
    total = sum((s + pltpu.roll(s, 96, 1)) * pltpu.roll(f, 64, 1) for s, f in zip(stats, factors))
    out = sum(n * spread(f, 0) for n, f in zip(numers, factors))
    return peak, total, out


def pack(peak, total):
    lead = rounded(total)
    rest = rounded(total - lead)
    lane = iota(peak.shape, 1)
    return jnp.where(lane < 64, peak, jnp.where(lane < 96, lead, pltpu.roll(rest, 32, 1)))


class Place:
    def __init__(self, sizes):
        self.Z, self.Y, self.C, self.T = sizes
        ctx = lax.axis_index("ctx")
        self.c = lax.rem(ctx, self.C)
        self.y = lax.rem(ctx // self.C, self.Y)
        self.z = ctx // (self.C * self.Y)
        self.ctx = ctx
        self.tp = lax.axis_index("tp")

    def z_at(self, k):
        return lax.rem(self.z + k + self.Z, self.Z)

    def y_at(self, k):
        return lax.rem(self.y + k + self.Y, self.Y)

    def tp_at(self, k):
        return lax.rem(self.tp + k + self.T, self.T)

    def ctx_of(self, z, y, c):
        return (z * self.Y + y) * self.C + c

    def copy(self, src, dst, send, recv, **axis):
        return pltpu.make_async_remote_copy(
            src_ref=src, dst_ref=dst, send_sem=send, recv_sem=recv, device_id=axis, device_id_type=MESH
        )


class Gather:
    def __init__(self, place, part, sems):
        self.p, self.part, self.H = place, part, place.Z // 2
        self.zz, self.ys, self.yr = sems
        self.half = place.z // self.H

    def z_copy(self, to, group):
        p = self.p
        block = self.part(p.y).at[p.z]
        return p.copy(block, block, self.zz.at[0, group], self.zz.at[1, group], ctx=p.ctx_of(to, p.y, p.c))

    def z_all(self, group):
        p = self.p
        block = self.part(p.y).at[pl.ds(0, self.H - 1 + group)]
        return p.copy(block, block, self.zz.at[0, group], self.zz.at[1, group], ctx=p.ctx_of(p.z_at(1), p.y, p.c))

    def half_at(self, group):
        return self.half if group == 0 else 1 - self.half

    def rows(self, group):
        return pl.ds(self.half_at(group) * self.H, self.H)

    def y_copy(self, k, group, send):
        p = self.p
        block = self.part(p.y if send else p.y_at(-k)).at[self.rows(group)]
        return p.copy(block, block, self.ys.at[group, k - 1], self.yr.at[group, k - 1], ctx=p.ctx_of(p.z, p.y_at(k), p.c))

    def start(self):
        H = self.H
        loop(0, H, lambda j: self.z_copy((1 - self.half) * H + lax.rem(self.p.z + j, H), 1).start())
        loop(1, H, lambda j: self.z_copy(self.half * H + lax.rem(self.p.z + j, H), 0).start())

    def along_y(self, group, order):
        if self.H - 1 + group:
            self.z_all(group).wait_recv()
        for k in order:
            self.y_copy(k, group, True).start()

    def arrived(self, k):
        for group in range(2):
            self.y_copy(k, group, False).wait_recv()

    def drain(self):
        for group in range(2):
            if self.H - 1 + group:
                self.z_all(group).wait_send()
            for k in range(1, self.p.Y):
                self.y_copy(k, group, True).wait_send()


def kernel(sizes, q_hbm, k_hbm, v_hbm, nk_hbm, nv_hbm, w_hbm, o_ref,
           kbuf, vbuf, vt, wbuf, qin, nkin, nvin, nkb, nvb, qrow, qbuf, qd, sbuf, pbuf, nb, st,
           ysb, yrb, zf, zsb, zss, zrb, zrs, abuf, af, pf, tf, ts, tr, of,
           ld, qsems, csems, asems, wsem, ry, rz, tt):
    p = Place(sizes)
    Z, Y, C, T = sizes
    z, y, c = p.z, p.y, p.c
    slots = C * Z
    rows = slots * HEADS
    near = [k for k in (1, 3, 2) if k < Y]
    units = [k for k in (2, 1, 3) if k < Y]

    def unit_at(i):
        return lax.rem(i, 2) * 2 + i // 2 if Y == 4 else i

    small = [pltpu.make_async_copy(a, b, ld.at[i]) for i, (a, b) in enumerate(((q_hbm, qin), (nk_hbm, nkin), (nv_hbm, nvin)))]
    w_load = pltpu.make_async_copy(w_hbm, wbuf.at[c], ld.at[3])

    def kv_load(s):
        return (pltpu.make_async_copy(k_hbm.at[s], kbuf.at[s], ld.at[4 + 2 * s]),
                pltpu.make_async_copy(v_hbm.at[s], vbuf.at[s], ld.at[5 + 2 * s]))

    for copy in small:
        copy.start()
    barrier = pltpu.get_barrier_semaphore()

    def greet(**axis):
        pl.semaphore_signal(barrier, inc=1, device_id=axis, device_id_type=MESH)

    def greet_tp(k):
        for cc in range(C):
            greet(ctx=p.ctx_of(z, y, cc), tp=p.tp_at(k))

    loop(1, Z, lambda k: greet(ctx=p.ctx_of(p.z_at(k), y, c)))
    for k in range(1, Y):
        for cc in range(C):
            greet(ctx=p.ctx_of(z, p.y_at(k), cc))
    greet(ctx=p.ctx_of(z, y, 1 - c))
    loop(1, T, greet_tp)
    for copy in [kv_load(s)[i] for i in (1, 0) for s in range(SEQS)]:
        copy.start()
    w_load.start()

    for copy in small:
        copy.wait()
    own = qin[...].astype(F32)
    for s in range(SEQS):
        for hd in range(HEADS):
            qrow[s * HEADS + hd:s * HEADS + hd + 1, :] = own[s:s + 1, hd * HD:(hd + 1) * HD]
    qbuf[y, c, z] = qrow[...].astype(BF16)
    qg = Gather(p, lambda yy: qbuf.at[yy, c], qsems)
    ag = Gather(p, lambda yy: abuf.at[yy], asems)
    pl.semaphore_wait(barrier, (Z - 1) + (Y * C - 1) + (T - 1) * C)
    qg.start()
    nk, nv = nkin[...].astype(F32), nvin[...].astype(F32)
    for s in range(SEQS):
        nkb[s] = jnp.broadcast_to(nk[s:s + 1], (PAD, HD)).astype(BF16)
        nvb[s] = jnp.broadcast_to(nv[s:s + 1], (8, HD))
    for pr in range(SEQS // 2):
        qd[pr] = jnp.zeros((2 * HD, 2 * rows), BF16)
        vt[pr, 2 * HD:, :] = jnp.ones((PAD, kbuf.shape[1]), BF16)

    def transpose(s):
        kv_load(s)[1].wait()
        at = pl.multiple_of(lax.rem(s, 2) * HD, HD)
        vt[s // 2, pl.ds(at, HD), :] = vbuf[s].T

    def attend(k):
        block = p.y_at(-k)
        x = qbuf[block].astype(F32).reshape(slots, SEQS, HEADS, HD)
        for s in range(SEQS):
            j = s % 2
            qd[s // 2, j * HD:(j + 1) * HD, j * rows:(j + 1) * rows] = x[:, s].reshape(rows, HD).T.astype(BF16)
        slot = lax.div(lax.rem(iota((8, 2 * rows), 1), rows), HEADS)
        token = lax.rem(slot, Z) * (Y * C) + block * C + lax.div(slot, Z)
        visible = token >= p.ctx
        chunk = min(CHUNK, kbuf.shape[1])
        chunks = [slice(a, a + chunk) for a in range(0, kbuf.shape[1], chunk)]

        def score(pr, at):
            keys = jnp.concatenate([kbuf[2 * pr, at], kbuf[2 * pr + 1, at]], axis=1)
            raw = jnp.dot(keys, qd[pr], preferred_element_type=F32)
            sbuf[pr, at] = raw
            return jnp.max(raw.reshape(chunk // 8, 8, 2 * rows), axis=0)

        def peak_of(pr, tops):
            keys = jnp.concatenate([nkb[2 * pr], nkb[2 * pr + 1]], axis=1)
            fresh = jnp.dot(keys, qd[pr], preferred_element_type=F32)[:8]
            fresh = jnp.where(visible, fresh, -jnp.inf)
            top = jnp.max(functools.reduce(jnp.maximum, tops + [fresh]), axis=0, keepdims=True)
            peak = rounded(top * SCALE)
            return peak, jnp.exp2(fresh * SCALE - peak)

        def weigh(pr, at, peak):
            pbuf[pr, at] = jnp.exp2(sbuf[pr, at] * SCALE - peak).astype(BF16)

        def finish(pr, peak, fresh):
            out = jnp.dot(vt[pr], pbuf[pr], preferred_element_type=F32)
            sub = iota((8, 2 * rows), 0)
            total = out[2 * HD:2 * HD + 8] + fresh
            three = jnp.where(sub == 0, peak, jnp.where(sub == 1, total, fresh))
            lane = iota((rows, HD), 1)
            row = iota((rows, HD), 0)
            for j in range(2):
                s = 2 * pr + j
                at = slice(j * rows, (j + 1) * rows)
                numer = out[j * HD:(j + 1) * HD, at].T
                cols = three[:, at].T
                numer = numer + rounded(cols[:, 2:3]) * nvb[s][:1]
                lead = rounded(cols[:, 1:2])
                rest = rounded(cols[:, 1:2] - lead)
                head = lax.rem(row, HEADS) + s * HEADS
                entry = jnp.where(lane == head, cols[:, 0:1], jnp.where(lane == head + 64, lead, jnp.where(lane == head + 96, rest, 0.0)))
                packed = jnp.sum(entry.reshape(slots, HEADS, HD), axis=1).reshape(C, Z, HD)
                st[k] = packed if s == 0 else st[k] + packed
                nb[k, :, :, s * HEADS:(s + 1) * HEADS, :] = numer.reshape(C, Z, HEADS, HD)

        tops = [score(0, at) for at in chunks]
        first = peak_of(0, tops)
        tops = []
        for at in chunks:
            tops.append(score(1, at))
            weigh(0, at, first[0])
        second = peak_of(1, tops)
        finish(0, *first)
        for at in chunks:
            weigh(1, at, second[0])
        finish(1, *second)

    def c_copy(k, group, send):
        block = qbuf.at[p.y_at(-k), c if send else 1 - c, qg.rows(group)]
        return p.copy(block, block, csems.at[0, group, k], csems.at[1, group, k], ctx=p.ctx_of(z, y, 1 - c))

    def w_copy():
        return p.copy(wbuf.at[c], wbuf.at[c], wsem.at[0], wsem.at[1], ctx=p.ctx_of(z, y, 1 - c))

    def core_at(j):
        return c if j == 0 else 1 - c

    def y_copy(k, j):
        dev = p.ctx_of(z, p.y_at(-k), core_at(j))
        return p.copy(ysb.at[k, j], yrb.at[k, j], ry.at[0, k, j], ry.at[1, k, j], ctx=dev)

    def z_copies(k):
        to = p.z_at(k)
        dev = p.ctx_of(to, y, c)
        return (p.copy(zsb.at[to], zrb.at[k - 1], rz.at[0, 0], rz.at[1, 0], ctx=dev),
                p.copy(zss.at[to], zrs.at[k - 1], rz.at[0, 1], rz.at[1, 1], ctx=dev))

    def z_all():
        dev = p.ctx_of(p.z_at(1), y, c)
        return (p.copy(zrb, zrb, rz.at[0, 0], rz.at[1, 0], ctx=dev), p.copy(zrs, zrs, rz.at[0, 1], rz.at[1, 1], ctx=dev))

    def t_copy(k, j):
        to = p.tp_at(k)
        return p.copy(ts.at[to * C + core_at(j)], tr.at[k * C + j], tt.at[0], tt.at[1], ctx=p.ctx_of(z, y, core_at(j)), tp=to)

    def t_all():
        block = tr.at[pl.ds(1, T * C - 1)]
        return p.copy(block, block, tt.at[0], tt.at[1], ctx=p.ctx_of(z, y, 1 - c))

    def message(stats, numer):
        pad = jnp.concatenate([stats, jnp.zeros((PAD - Z, HD), F32)], axis=0)
        return jnp.concatenate([numer.reshape(Z * UNIT, HD), pad], axis=0).astype(BF16)

    def reduce_y(k):
        ysb[k, 1] = message(st[k, 1 - c], nb[k, 1 - c])
        y_copy(k, 1).start()

        @pl.when(k > 0)
        def _():
            ysb[k, 0] = message(st[k, c], nb[k, c])
            y_copy(k, 0).start()

    def received(k, j):
        y_copy(k, j).wait_recv()
        got = yrb[k, j].astype(F32)
        return got[Z * UNIT:Z * UNIT + Z], got[:Z * UNIT].reshape(Z, UNIT, HD)

    def reduce_z():
        early = [(st[0, c], nb[0, c]), received(0, 1)] + [received(k, j) for k in units[:-1] for j in range(C)]
        peak, total, numer = merge(*zip(*early))
        late = [(pack(peak, total), numer)] + [received(units[-1], j) for j in range(C)]
        peak, total, numer = merge(*zip(*late))
        stats = pack(peak, total)
        zsb[...] = numer.astype(BF16)
        for k in range(Z):
            zss[k] = stats[k:k + 1]

        def send(k):
            for copy in z_copies(k):
                copy.start()
        loop(1, Z, send)
        zf[...] = numer

    def attended():
        stats, numers = [zss[z]], [zf[z][None]]
        for copy in z_all():
            copy.wait_recv()
        for k in range(Z - 1):
            stats.append(zrs[k])
            numers.append(zrb[k].astype(F32)[None])
        peak, total, numer = merge(stats, numers)
        abuf[y, z] = (numer / spread(total, 64))[0].astype(BF16)

    def project(k):
        block = p.y_at(-k)
        af[...] = abuf[block].reshape(Z * UNIT, HD).astype(F32)
        n = Z * SEQS
        heads = [af[pl.ds(hd, n, stride=HEADS), :].astype(BF16) for hd in range(HEADS)]
        at = pl.multiple_of(block * n, n)
        both = jnp.dot(jnp.concatenate(heads, axis=1), jnp.concatenate([wbuf[0], wbuf[1]], axis=1), preferred_element_type=F32)
        for cc in range(C):
            pf[cc, pl.ds(at, n), :] = both[:, cc * HD:(cc + 1) * HD]

    loop(0, SEQS // 2, transpose)
    for group in range(2):
        qg.along_y(group, units)
        c_copy(0, group, True).start()
    w_load.wait()
    w_copy().start()
    loop(SEQS // 2, SEQS, transpose)
    loop(0, SEQS, lambda s: kv_load(s)[0].wait())

    def unit(i):
        k = unit_at(i)
        for group in range(2):
            c_copy(k, group, False).wait_recv()
        attend(k)
        reduce_y(k)

        @pl.when(i == 0)
        def _():
            for k in near:
                qg.arrived(k)
                for group in range(2):
                    c_copy(k, group, True).start()

    loop(0, Y, unit)
    reduce_z()
    attended()
    ag.start()
    w_copy().wait_recv()
    for group in range(2):
        ag.along_y(group, units)
    for k in [0] + near:
        if k:
            ag.arrived(k)
        project(k)
    for t in range(T):
        for cc in range(C):
            tile = [pf[cc, pl.ds(SEQS * t + s, Y, stride=SEQS * Z), :] for s in range(SEQS)]
            tile = jnp.concatenate(tile, axis=0)
            tf[t * C + cc] = tile
            ts[t * C + cc] = tile.astype(BF16)

    def send(k):
        for j in range(C):
            t_copy(k, j).start()

    loop(1, T, send)
    t_copy(0, 1).start()
    mine = tf[p.tp * C + c]
    t_all().wait_recv()
    for k in range(1, T):
        mine = mine + tr[k * C].astype(F32)
    other = sum(tr[k * C + 1].astype(F32) for k in range(T))
    for s in range(SEQS):
        of[pl.ds(s * Y * C + c, Y, stride=C), :] = mine[s * Y:(s + 1) * Y]
        of[pl.ds(s * Y * C + 1 - c, Y, stride=C), :] = other[s * Y:(s + 1) * Y]
    o_ref[...] = of[...].astype(BF16)

    qg.drain()
    ag.drain()
    w_copy().wait_send()
    for k in range(Y):
        for group in range(2):
            c_copy(k, group, True).wait_send()
        for j in range(C):
            if k + j:
                y_copy(k, j).wait_send()
    for copy in z_all():
        copy.wait_send()
    t_all().wait_send()


def build(sizes, queries, keys, values, new_keys, new_values, weight):
    Z, Y, C, T = sizes
    S = keys.shape[1]
    V = pltpu.VMEM
    dma = pltpu.SemaphoreType.DMA
    slots = C * Z
    rows = slots * HEADS
    out_rows = SEQS * Y * C
    block = Z * UNIT + PAD
    tile = SEQS * Y
    scratch = [
        V((SEQS, S, HD), BF16), V((SEQS, S, HD), BF16), V((SEQS // 2, 2 * HD + PAD, S), BF16), V((C,) + weight.shape, BF16),
        V((SEQS, HEADS * HD), BF16), V((SEQS, HD), BF16), V((SEQS, HD), BF16),
        V((SEQS, PAD, HD), BF16), V((SEQS, 8, HD), F32), V((UNIT, HD), F32),
        V((Y, C, Z, UNIT, HD), BF16), V((SEQS // 2, 2 * HD, 2 * rows), BF16),
        V((SEQS // 2, S, 2 * rows), F32), V((SEQS // 2, S, 2 * rows), BF16),
        V((Y, C, Z, UNIT, HD), F32), V((Y, C, Z, HD), F32),
        V((Y, C, block, HD), BF16), V((Y, C, block, HD), BF16),
        V((Z, UNIT, HD), F32), V((Z, UNIT, HD), BF16), V((Z, 1, HD), F32),
        V((Z - 1, UNIT, HD), BF16), V((Z - 1, 1, HD), F32),
        V((Y, Z, UNIT, HD), BF16), V((Z * UNIT, HD), F32), V((C, Y * Z * SEQS, HD), F32),
        V((T * C, tile, HD), F32), V((T * C, tile, HD), BF16), V((T * C, tile, HD), BF16), V((out_rows, HD), F32),
        dma((4 + 2 * SEQS,)), [dma((2, 2)), dma((2, Y - 1)), dma((2, Y - 1))], dma((2, 2, Y)),
        [dma((2, 2)), dma((2, Y - 1)), dma((2, Y - 1))], dma((2,)), dma((2, Y, C)), dma((2, 2)), dma((2,)),
    ]
    out = pl.pallas_call(
        functools.partial(kernel, sizes),
        out_shape=jax.ShapeDtypeStruct((out_rows, HD), BF16),
        in_specs=[pl.BlockSpec(memory_space=pltpu.HBM)] * 6,
        out_specs=pl.BlockSpec(memory_space=pltpu.VMEM),
        scratch_shapes=scratch,
        compiler_params=pltpu.CompilerParams(
            collective_id=0, has_side_effects=True, vmem_limit_bytes=64 * 1024 * 1024
        ),
        cost_estimate=pl.CostEstimate(
            flops=4 * SEQS * Y * rows * S * HD, bytes_accessed=4 * SEQS * S * HD,
            transcendentals=SEQS * Y * rows * S,
        ),
    )(
        queries.reshape(SEQS, HEADS * HD), keys, values,
        new_keys.reshape(SEQS, HD), new_values.reshape(SEQS, HD), weight,
    )
    return out.reshape(SEQS, Y * C, HD)


def solution(mesh):
    Z = mesh.shape["tp"]
    sizes = (Z, mesh.shape["ctx"] // (2 * Z), 2, mesh.shape["tp"])
    spec = P(None, "ctx", "tp")
    return jax.shard_map(
        functools.partial(build, sizes),
        mesh=mesh,
        in_specs=(spec, spec, spec, spec, spec, P("tp", "ctx")),
        out_specs=P(None, "tp", "ctx"),
        check_vma=False,
    )
```

```python
import functools
import math

import jax
import jax.numpy as jnp
from jax import lax
from jax.experimental import pallas as pl
from jax.experimental.pallas import tpu as pltpu
from jax.sharding import PartitionSpec as P

HD = 128
HEADS = 8
SEQS = 4
UNIT = SEQS * HEADS
PAD = 16
CHUNK = 256
SCALE = math.log2(math.e) / math.sqrt(HD)
MESH = pl.DeviceIdType.MESH
F32 = jnp.float32
BF16 = jnp.bfloat16


def iota(shape, dim):
    return lax.broadcasted_iota(jnp.int32, shape, dim)


def loop(first, last, body):
    lax.fori_loop(first, last, lambda i, c: (body(i), c)[1], 0)


def rounded(x):
    return x.astype(BF16).astype(F32)


def spread(packed, first):
    shape = (packed.shape[0], UNIT, HD)
    wide = jnp.broadcast_to(packed[:, None, :], shape)
    hit = iota(shape, 2) == iota(shape, 1) + first
    return jnp.sum(jnp.where(hit, wide, 0.0), axis=-1, keepdims=True)


def merge(stats, numers):
    peak = functools.reduce(jnp.maximum, stats)
    factors = [jnp.exp2(s - peak) for s in stats]
    total = sum((s + pltpu.roll(s, 96, 1)) * pltpu.roll(f, 64, 1) for s, f in zip(stats, factors))
    out = sum(n * spread(f, 0) for n, f in zip(numers, factors))
    return peak, total, out


def pack(peak, total):
    lead = rounded(total)
    rest = rounded(total - lead)
    lane = iota(peak.shape, 1)
    return jnp.where(lane < 64, peak, jnp.where(lane < 96, lead, pltpu.roll(rest, 32, 1)))


class Place:
    def __init__(self, sizes):
        self.Z, self.Y, self.C, self.T = sizes
        ctx = lax.axis_index("ctx")
        self.c = lax.rem(ctx, self.C)
        self.y = lax.rem(ctx // self.C, self.Y)
        self.z = ctx // (self.C * self.Y)
        self.ctx = ctx
        self.tp = lax.axis_index("tp")
        self.X = self.T // 2
        self.x = self.tp // 2
        self.hi = lax.rem(self.tp, 2)

    def z_at(self, k):
        return lax.rem(self.z + k + self.Z, self.Z)

    def y_at(self, k):
        return lax.rem(self.y + k + self.Y, self.Y)

    def x_at(self, k):
        return lax.rem(self.x + k + self.X, self.X)

    def ctx_of(self, z, y, c):
        return (z * self.Y + y) * self.C + c

    def copy(self, src, dst, send, recv, **axis):
        return pltpu.make_async_remote_copy(
            src_ref=src, dst_ref=dst, send_sem=send, recv_sem=recv, device_id=axis, device_id_type=MESH
        )


class Gather:
    def __init__(self, place, part, sems):
        self.p, self.part, self.H = place, part, place.Z // 2
        self.zz, self.ys, self.yr = sems
        self.half = place.z // self.H

    def z_copy(self, to, group):
        p = self.p
        block = self.part(p.y).at[p.z]
        return p.copy(block, block, self.zz.at[0, group], self.zz.at[1, group], ctx=p.ctx_of(to, p.y, p.c))

    def z_all(self, group):
        p = self.p
        block = self.part(p.y).at[pl.ds(0, self.H - 1 + group)]
        return p.copy(block, block, self.zz.at[0, group], self.zz.at[1, group], ctx=p.ctx_of(p.z_at(1), p.y, p.c))

    def half_at(self, group):
        return self.half if group == 0 else 1 - self.half

    def rows(self, group):
        return pl.ds(self.half_at(group) * self.H, self.H)

    def y_copy(self, k, group, send):
        p = self.p
        block = self.part(p.y if send else p.y_at(-k)).at[self.rows(group)]
        return p.copy(block, block, self.ys.at[group, k - 1], self.yr.at[group, k - 1], ctx=p.ctx_of(p.z, p.y_at(k), p.c))

    def start(self):
        H = self.H
        loop(0, H, lambda j: self.z_copy((1 - self.half) * H + lax.rem(self.p.z + j, H), 1).start())
        loop(1, H, lambda j: self.z_copy(self.half * H + lax.rem(self.p.z + j, H), 0).start())

    def z_arrived(self, group):
        if self.H - 1 + group:
            self.z_all(group).wait_recv()

    def along_y(self, group, order):
        for k in order:
            self.y_copy(k, group, True).start()

    def arrived(self, k):
        for group in range(2):
            self.y_copy(k, group, False).wait_recv()

    def drain(self, z_too):
        for group in range(2):
            if z_too and self.H - 1 + group:
                self.z_all(group).wait_send()
            for k in range(1, self.p.Y):
                self.y_copy(k, group, True).wait_send()


def kernel(sizes, q_hbm, k_hbm, v_hbm, nk_hbm, nv_hbm, w_hbm, o_ref,
           kbuf, vbuf, vt, wbuf, qin, nkin, nvin, nkb, nvb, qrow, qbuf, qd, sbuf, pbuf, nb, st,
           ysb, yrb, zsb, zss, zrb, zrs, abuf, af, pf, tf, ts, tr, us, ur, of,
           ld, qsems, csems, asems, wsem, ry, rz, az, tt, uu):
    p = Place(sizes)
    Z, Y, C, T = sizes
    z, y, c = p.z, p.y, p.c
    slots = C * Z
    rows = slots * HEADS
    near = [k for k in (1, 3, 2) if k < Y]
    units = [k for k in (2, 1, 3) if k < Y]

    def unit_at(i):
        return lax.rem(i, 2) * 2 + i // 2 if Y == 4 else i

    small = [pltpu.make_async_copy(a, b, ld.at[i]) for i, (a, b) in enumerate(((q_hbm, qin), (nk_hbm, nkin), (nv_hbm, nvin)))]
    w_load = pltpu.make_async_copy(w_hbm, wbuf.at[c], ld.at[3])

    def kv_load(s):
        return (pltpu.make_async_copy(k_hbm.at[s], kbuf.at[s], ld.at[4 + 2 * s]),
                pltpu.make_async_copy(v_hbm.at[s], vbuf.at[s], ld.at[5 + 2 * s]))

    for copy in small:
        copy.start()
    barrier = pltpu.get_barrier_semaphore()

    def greet(**axis):
        pl.semaphore_signal(barrier, inc=1, device_id=axis, device_id_type=MESH)

    loop(1, Z, lambda k: greet(ctx=p.ctx_of(p.z_at(k), y, c)))
    for k in range(1, Y):
        for cc in range(C):
            greet(ctx=p.ctx_of(z, p.y_at(k), cc))
    greet(ctx=p.ctx_of(z, y, 1 - c))
    for k in range(1, p.X):
        greet(tp=p.x_at(k) * 2 + p.hi)
    for cc in range(C):
        greet(ctx=p.ctx_of(z, y, cc), tp=p.x * 2 + 1 - p.hi)
    for copy in [kv_load(s)[i] for i in (1, 0) for s in range(SEQS)]:
        copy.start()
    w_load.start()

    for copy in small:
        copy.wait()
    own = qin[...].astype(F32)
    for s in range(SEQS):
        for hd in range(HEADS):
            qrow[s * HEADS + hd:s * HEADS + hd + 1, :] = own[s:s + 1, hd * HD:(hd + 1) * HD]
    qbuf[y, c, z] = qrow[...].astype(BF16)
    qg = Gather(p, lambda yy: qbuf.at[yy, c], qsems)
    ag = Gather(p, lambda yy: abuf.at[yy], asems)
    pl.semaphore_wait(barrier, (Z - 1) + (Y * C - 1) + (p.X - 1) + C)
    qg.start()
    nk, nv = nkin[...].astype(F32), nvin[...].astype(F32)
    for s in range(SEQS):
        nkb[s] = jnp.broadcast_to(nk[s:s + 1], (PAD, HD)).astype(BF16)
        nvb[s] = jnp.broadcast_to(nv[s:s + 1], (8, HD))
    for pr in range(SEQS // 2):
        qd[pr] = jnp.zeros((2 * HD, 2 * rows), BF16)
        vt[pr, 2 * HD:, :] = jnp.ones((PAD, kbuf.shape[1]), BF16)

    def transpose(s):
        kv_load(s)[1].wait()
        at = pl.multiple_of(lax.rem(s, 2) * HD, HD)
        vt[s // 2, pl.ds(at, HD), :] = vbuf[s].T

    def attend(k):
        block = p.y_at(-k)
        x = qbuf[block].astype(F32).reshape(slots, SEQS, HEADS, HD)
        for s in range(SEQS):
            j = s % 2
            qd[s // 2, j * HD:(j + 1) * HD, j * rows:(j + 1) * rows] = x[:, s].reshape(rows, HD).T.astype(BF16)
        slot = lax.div(lax.rem(iota((8, 2 * rows), 1), rows), HEADS)
        token = lax.rem(slot, Z) * (Y * C) + block * C + lax.div(slot, Z)
        visible = token >= p.ctx
        chunk = min(CHUNK, kbuf.shape[1])
        chunks = [slice(a, a + chunk) for a in range(0, kbuf.shape[1], chunk)]

        def score(pr, at):
            keys = jnp.concatenate([kbuf[2 * pr, at], kbuf[2 * pr + 1, at]], axis=1)
            raw = jnp.dot(keys, qd[pr], preferred_element_type=F32)
            sbuf[pr, at] = raw
            return jnp.max(raw.reshape(chunk // 8, 8, 2 * rows), axis=0)

        def peak_of(pr, tops):
            keys = jnp.concatenate([nkb[2 * pr], nkb[2 * pr + 1]], axis=1)
            fresh = jnp.dot(keys, qd[pr], preferred_element_type=F32)[:8]
            fresh = jnp.where(visible, fresh, -jnp.inf)
            top = jnp.max(functools.reduce(jnp.maximum, tops + [fresh]), axis=0, keepdims=True)
            peak = rounded(top * SCALE)
            return peak, jnp.exp2(fresh * SCALE - peak)

        def weigh(pr, at, peak):
            pbuf[pr, at] = jnp.exp2(sbuf[pr, at] * SCALE - peak).astype(BF16)

        def finish(pr, peak, fresh):
            out = jnp.dot(vt[pr], pbuf[pr], preferred_element_type=F32)
            sub = iota((8, 2 * rows), 0)
            total = out[2 * HD:2 * HD + 8] + fresh
            three = jnp.where(sub == 0, peak, jnp.where(sub == 1, total, fresh))
            lane = iota((rows, HD), 1)
            row = iota((rows, HD), 0)
            for j in range(2):
                s = 2 * pr + j
                at = slice(j * rows, (j + 1) * rows)
                numer = out[j * HD:(j + 1) * HD, at].T
                cols = three[:, at].T
                numer = numer + rounded(cols[:, 2:3]) * nvb[s][:1]
                lead = rounded(cols[:, 1:2])
                rest = rounded(cols[:, 1:2] - lead)
                head = lax.rem(row, HEADS) + s * HEADS
                entry = jnp.where(lane == head, cols[:, 0:1], jnp.where(lane == head + 64, lead, jnp.where(lane == head + 96, rest, 0.0)))
                packed = jnp.sum(entry.reshape(slots, HEADS, HD), axis=1).reshape(C, Z, HD)
                st[k] = packed if s == 0 else st[k] + packed
                nb[k, :, :, s * HEADS:(s + 1) * HEADS, :] = numer.reshape(C, Z, HEADS, HD)

        tops = [score(0, at) for at in chunks]
        first = peak_of(0, tops)
        tops = []
        for at in chunks:
            tops.append(score(1, at))
            weigh(0, at, first[0])
        second = peak_of(1, tops)
        finish(0, *first)
        for at in chunks:
            weigh(1, at, second[0])
        finish(1, *second)

    def c_copy(k, group, send):
        block = qbuf.at[p.y_at(-k), c if send else 1 - c, qg.rows(group)]
        return p.copy(block, block, csems.at[0, group, k], csems.at[1, group, k], ctx=p.ctx_of(z, y, 1 - c))

    def w_copy():
        return p.copy(wbuf.at[c], wbuf.at[c], wsem.at[0], wsem.at[1], ctx=p.ctx_of(z, y, 1 - c))

    def core_at(j):
        return c if j == 0 else 1 - c

    def y_copy(k, j):
        dev = p.ctx_of(z, p.y_at(-k), core_at(j))
        return p.copy(ysb.at[k, j], yrb.at[k, j], ry.at[0, k, j], ry.at[1, k, j], ctx=dev)

    owners = Z // 2
    mine = z - Z // 4
    owner = (mine >= 0) & (mine < owners)

    def z_copies(o, index):
        dev = p.ctx_of(Z // 4 + o, y, c)
        at = pl.ds(2 * o, 2)
        return (p.copy(zsb.at[at], zrb.at[index], rz.at[0, 0, o], rz.at[1, 0, index], ctx=dev),
                p.copy(zss.at[at], zrs.at[index], rz.at[0, 1, o], rz.at[1, 1, index], ctx=dev))

    def others(last, here, body):
        def one(i):
            @pl.when(i != here)
            def _():
                body(i)
        loop(0, last, one)

    def a_copy(to, o):
        block = abuf.at[y, pl.ds(2 * o, 2)]
        return p.copy(block, block, az.at[0, to], az.at[1, o], ctx=p.ctx_of(to, y, c))

    def t_copy(k):
        to = p.x_at(k)
        return p.copy(ts.at[to], tr.at[k - 1], tt.at[0, k - 1], tt.at[1, k - 1], tp=to * 2 + p.hi)

    def u_copy(dh, dc):
        hi, cc = (1 - p.hi if dh else p.hi), core_at(dc)
        i = dh * C + dc
        return p.copy(us.at[hi * C + cc], ur.at[i], uu.at[0, i], uu.at[1, i], ctx=p.ctx_of(z, y, cc), tp=p.x * 2 + hi)

    corners = [(1, 0), (1, 1), (0, 1)]

    def message(stats, numer):
        pad = jnp.concatenate([stats, jnp.zeros((PAD - Z, HD), F32)], axis=0)
        return jnp.concatenate([numer.reshape(Z * UNIT, HD), pad], axis=0).astype(BF16)

    def reduce_y(k):
        ysb[k, 1] = message(st[k, 1 - c], nb[k, 1 - c])
        y_copy(k, 1).start()

        @pl.when(k > 0)
        def _():
            ysb[k, 0] = message(st[k, c], nb[k, c])
            y_copy(k, 0).start()

    def received(k, j):
        y_copy(k, j).wait_recv()
        got = yrb[k, j].astype(F32)
        return got[Z * UNIT:Z * UNIT + Z], got[:Z * UNIT].reshape(Z, UNIT, HD)

    def reduce_z():
        early = [(st[0, c], nb[0, c]), received(0, 1)] + [received(k, j) for k in units[:-1] for j in range(C)]
        peak, total, numer = merge(*zip(*early))
        late = [(pack(peak, total), numer)] + [received(units[-1], j) for j in range(C)]
        peak, total, numer = merge(*zip(*late))
        stats = pack(peak, total)
        zsb[...] = numer.astype(BF16)
        for k in range(Z):
            zss[k] = stats[k:k + 1]

        def send(o):
            for copy in z_copies(o, z):
                copy.start()
        others(owners, mine, send)

    def attended():
        at = pl.ds(2 * mine, 2)
        zrb[z] = zsb[at]
        zrs[z] = zss[at]

        def wait(i):
            for copy in z_copies(mine, i):
                copy.wait_recv()
        others(Z, z, wait)
        stats = [jnp.concatenate([zrs[i, 0], zrs[i, 1]], axis=0) for i in range(Z)]
        peak, total, numer = merge(stats, [zrb[i].astype(F32) for i in range(Z)])
        abuf[y, at] = (numer / spread(total, 64)).astype(BF16)
        others(Z, z, lambda to: a_copy(to, mine).start())

    def project(k):
        block = p.y_at(-k)
        af[...] = abuf[block].reshape(Z * UNIT, HD).astype(F32)
        n = Z * SEQS
        heads = [af[pl.ds(hd, n, stride=HEADS), :].astype(BF16) for hd in range(HEADS)]
        at = pl.multiple_of(block * n, n)
        both = jnp.dot(jnp.concatenate(heads, axis=1), jnp.concatenate([wbuf[0], wbuf[1]], axis=1), preferred_element_type=F32)
        for cc in range(C):
            pf[cc, pl.ds(at, n), :] = both[:, cc * HD:(cc + 1) * HD]

    loop(0, SEQS // 2, transpose)
    for group in range(2):
        qg.z_arrived(group)
        c_copy(0, group, True).start()
        qg.along_y(group, units)
    w_load.wait()
    w_copy().start()
    loop(SEQS // 2, SEQS, transpose)
    loop(0, SEQS, lambda s: kv_load(s)[0].wait())

    def unit(i):
        k = unit_at(i)
        for group in range(2):
            c_copy(k, group, False).wait_recv()
        attend(k)
        reduce_y(k)

        @pl.when(i == 0)
        def _():
            for k in near:
                qg.arrived(k)
                for group in range(2):
                    c_copy(k, group, True).start()

    loop(0, Y, unit)
    reduce_z()
    pl.when(owner)(attended)
    w_copy().wait_recv()
    for group in range(2):
        for o in range(owners // 2):
            at = ag.half_at(group) * (owners // 2) + o

            @pl.when(at != mine)
            def _():
                a_copy(z, at).wait_recv()
        ag.along_y(group, units)
    for k in [0] + near:
        if k:
            ag.arrived(k)
        project(k)
    for t in range(T):
        for cc in range(C):
            tile = [pf[cc, pl.ds(SEQS * t + s, Y, stride=SEQS * Z), :] for s in range(SEQS)]
            tile = jnp.concatenate(tile, axis=0)
            tf[t // 2, t % 2 * C + cc] = tile
            ts[t // 2, t % 2 * C + cc] = tile.astype(BF16)
    for k in range(1, p.X):
        t_copy(k).start()
    total = tf[p.x]
    for k in range(1, p.X):
        t_copy(k).wait_recv()
        total = total + tr[k - 1].astype(F32)
    tf[p.x] = total
    us[...] = total.astype(BF16)
    for corner in corners:
        u_copy(*corner).start()
    same = tf[p.x, p.hi * C + c]
    u_copy(0, 1).wait_recv()
    other = ur[1].astype(F32)
    u_copy(1, 0).wait_recv()
    same = same + ur[C].astype(F32)
    u_copy(1, 1).wait_recv()
    other = other + ur[C + 1].astype(F32)
    for s in range(SEQS):
        of[pl.ds(s * Y * C + c, Y, stride=C), :] = same[s * Y:(s + 1) * Y]
        of[pl.ds(s * Y * C + 1 - c, Y, stride=C), :] = other[s * Y:(s + 1) * Y]
    o_ref[...] = of[...].astype(BF16)

    qg.drain(True)
    ag.drain(False)
    w_copy().wait_send()
    for k in range(Y):
        for group in range(2):
            c_copy(k, group, True).wait_send()
        for j in range(C):
            if k + j:
                y_copy(k, j).wait_send()

    def sent(o):
        for copy in z_copies(o, z):
            copy.wait_send()
    others(owners, mine, sent)

    @pl.when(owner)
    def _():
        others(Z, z, lambda to: a_copy(to, mine).wait_send())

    for k in range(1, p.X):
        t_copy(k).wait_send()
    for corner in corners:
        u_copy(*corner).wait_send()


def build(sizes, queries, keys, values, new_keys, new_values, weight):
    Z, Y, C, T = sizes
    S = keys.shape[1]
    V = pltpu.VMEM
    dma = pltpu.SemaphoreType.DMA
    slots = C * Z
    rows = slots * HEADS
    out_rows = SEQS * Y * C
    block = Z * UNIT + PAD
    tile = SEQS * Y
    X = T // 2
    scratch = [
        V((SEQS, S, HD), BF16), V((SEQS, S, HD), BF16), V((SEQS // 2, 2 * HD + PAD, S), BF16), V((C,) + weight.shape, BF16),
        V((SEQS, HEADS * HD), BF16), V((SEQS, HD), BF16), V((SEQS, HD), BF16),
        V((SEQS, PAD, HD), BF16), V((SEQS, 8, HD), F32), V((UNIT, HD), F32),
        V((Y, C, Z, UNIT, HD), BF16), V((SEQS // 2, 2 * HD, 2 * rows), BF16),
        V((SEQS // 2, S, 2 * rows), F32), V((SEQS // 2, S, 2 * rows), BF16),
        V((Y, C, Z, UNIT, HD), F32), V((Y, C, Z, HD), F32),
        V((Y, C, block, HD), BF16), V((Y, C, block, HD), BF16),
        V((Z, UNIT, HD), BF16), V((Z, 1, HD), F32),
        V((Z, 2, UNIT, HD), BF16), V((Z, 2, 1, HD), F32),
        V((Y, Z, UNIT, HD), BF16), V((Z * UNIT, HD), F32), V((C, Y * Z * SEQS, HD), F32),
        V((X, 2 * C, tile, HD), F32), V((X, 2 * C, tile, HD), BF16), V((max(X - 1, 1), 2 * C, tile, HD), BF16),
        V((2 * C, tile, HD), BF16), V((2 * C, tile, HD), BF16), V((out_rows, HD), F32),
        dma((4 + 2 * SEQS,)), [dma((2, 2)), dma((2, Y - 1)), dma((2, Y - 1))], dma((2, 2, Y)),
        [dma((2, 2)), dma((2, Y - 1)), dma((2, Y - 1))], dma((2,)), dma((2, Y, C)),
        dma((2, 2, Z)), dma((2, Z)), dma((2, max(X - 1, 1))), dma((2, 2 * C)),
    ]
    out = pl.pallas_call(
        functools.partial(kernel, sizes),
        out_shape=jax.ShapeDtypeStruct((out_rows, HD), BF16),
        in_specs=[pl.BlockSpec(memory_space=pltpu.HBM)] * 6,
        out_specs=pl.BlockSpec(memory_space=pltpu.VMEM),
        scratch_shapes=scratch,
        compiler_params=pltpu.CompilerParams(
            collective_id=0, has_side_effects=True, vmem_limit_bytes=64 * 1024 * 1024
        ),
        cost_estimate=pl.CostEstimate(
            flops=4 * SEQS * Y * rows * S * HD, bytes_accessed=4 * SEQS * S * HD,
            transcendentals=SEQS * Y * rows * S,
        ),
    )(
        queries.reshape(SEQS, HEADS * HD), keys, values,
        new_keys.reshape(SEQS, HD), new_values.reshape(SEQS, HD), weight,
    )
    return out.reshape(SEQS, Y * C, HD)


def solution(mesh):
    Z = mesh.shape["tp"]
    sizes = (Z, mesh.shape["ctx"] // (2 * Z), 2, mesh.shape["tp"])
    spec = P(None, "ctx", "tp")
    return jax.shard_map(
        functools.partial(build, sizes),
        mesh=mesh,
        in_specs=(spec, spec, spec, spec, spec, P("tp", "ctx")),
        out_specs=P(None, "tp", "ctx"),
        check_vma=False,
    )
```

```python
import functools
import math

import jax
import jax.numpy as jnp
from jax import lax
from jax.experimental import pallas as pl
from jax.experimental.pallas import tpu as pltpu
from jax.sharding import PartitionSpec as P

HD = 128
HEADS = 8
SEQS = 4
UNIT = SEQS * HEADS
PAD = 16
CHUNK = 256
SCALE = math.log2(math.e) / math.sqrt(HD)
MESH = pl.DeviceIdType.MESH
F32 = jnp.float32
BF16 = jnp.bfloat16


def iota(shape, dim):
    return lax.broadcasted_iota(jnp.int32, shape, dim)


def loop(first, last, body):
    lax.fori_loop(first, last, lambda i, c: (body(i), c)[1], 0)


def rounded(x):
    return x.astype(BF16).astype(F32)


def spread(packed, first):
    shape = (packed.shape[0], UNIT, HD)
    wide = jnp.broadcast_to(packed[:, None, :], shape)
    hit = iota(shape, 2) == iota(shape, 1) + first
    return jnp.sum(jnp.where(hit, wide, 0.0), axis=-1, keepdims=True)


def merge(stats, numers):
    peak = functools.reduce(jnp.maximum, stats)
    factors = [jnp.exp2(s - peak) for s in stats]
    total = sum((s + pltpu.roll(s, 96, 1)) * pltpu.roll(f, 64, 1) for s, f in zip(stats, factors))
    out = sum(n * spread(f, 0) for n, f in zip(numers, factors))
    return peak, total, out


def pack(peak, total):
    lead = rounded(total)
    rest = rounded(total - lead)
    lane = iota(peak.shape, 1)
    return jnp.where(lane < 64, peak, jnp.where(lane < 96, lead, pltpu.roll(rest, 32, 1)))


class Place:
    def __init__(self, sizes):
        self.Z, self.Y, self.C, self.T = sizes
        ctx = lax.axis_index("ctx")
        self.c = lax.rem(ctx, self.C)
        self.y = lax.rem(ctx // self.C, self.Y)
        self.z = ctx // (self.C * self.Y)
        self.ctx = ctx
        self.tp = lax.axis_index("tp")

    def z_at(self, k):
        return lax.rem(self.z + k + self.Z, self.Z)

    def y_at(self, k):
        return lax.rem(self.y + k + self.Y, self.Y)

    def tp_at(self, k):
        return lax.rem(self.tp + k + self.T, self.T)

    def ctx_of(self, z, y, c):
        return (z * self.Y + y) * self.C + c

    def copy(self, src, dst, send, recv, **axis):
        return pltpu.make_async_remote_copy(
            src_ref=src, dst_ref=dst, send_sem=send, recv_sem=recv, device_id=axis, device_id_type=MESH
        )


class Gather:
    def __init__(self, place, part, sems):
        self.p, self.part, self.H = place, part, place.Z // 2
        self.zz, self.ys, self.yr = sems
        self.half = place.z // self.H

    def z_copy(self, to, group):
        p = self.p
        block = self.part(p.y).at[p.z]
        return p.copy(block, block, self.zz.at[0, group], self.zz.at[1, group], ctx=p.ctx_of(to, p.y, p.c))

    def z_all(self, group):
        p = self.p
        block = self.part(p.y).at[pl.ds(0, self.H - 1 + group)]
        return p.copy(block, block, self.zz.at[0, group], self.zz.at[1, group], ctx=p.ctx_of(p.z_at(1), p.y, p.c))

    def half_at(self, group):
        return self.half if group == 0 else 1 - self.half

    def rows(self, group):
        return pl.ds(self.half_at(group) * self.H, self.H)

    def y_copy(self, k, group, send):
        p = self.p
        block = self.part(p.y if send else p.y_at(-k)).at[self.rows(group)]
        return p.copy(block, block, self.ys.at[group, k - 1], self.yr.at[group, k - 1], ctx=p.ctx_of(p.z, p.y_at(k), p.c))

    def start(self):
        H = self.H
        loop(0, H, lambda j: self.z_copy((1 - self.half) * H + lax.rem(self.p.z + j, H), 1).start())
        loop(1, H, lambda j: self.z_copy(self.half * H + lax.rem(self.p.z + j, H), 0).start())

    def z_arrived(self, group):
        if self.H - 1 + group:
            self.z_all(group).wait_recv()

    def along_y(self, group, order):
        for k in order:
            self.y_copy(k, group, True).start()

    def arrived(self, k):
        for group in range(2):
            self.y_copy(k, group, False).wait_recv()

    def drain(self, z_too):
        for group in range(2):
            if z_too and self.H - 1 + group:
                self.z_all(group).wait_send()
            for k in range(1, self.p.Y):
                self.y_copy(k, group, True).wait_send()


def kernel(sizes, q_hbm, k_hbm, v_hbm, nk_hbm, nv_hbm, w_hbm, o_ref,
           kbuf, vbuf, vt, wbuf, qin, nkin, nvin, nkb, nvb, qrow, qbuf, qd, sbuf, pbuf, nb, st,
           ysb, yrb, zsb, zss, zrb, zrs, abuf, af, pf, tf, ts, tr, of,
           ld, qsems, csems, asems, wsem, ry, rz, az, tt):
    p = Place(sizes)
    Z, Y, C, T = sizes
    z, y, c = p.z, p.y, p.c
    slots = C * Z
    rows = slots * HEADS
    near = [k for k in (1, 3, 2) if k < Y]
    units = [k for k in (2, 1, 3) if k < Y]

    def unit_at(i):
        return lax.rem(i, 2) * 2 + i // 2 if Y == 4 else i

    small = [pltpu.make_async_copy(a, b, ld.at[i]) for i, (a, b) in enumerate(((q_hbm, qin), (nk_hbm, nkin), (nv_hbm, nvin)))]
    w_load = pltpu.make_async_copy(w_hbm, wbuf.at[c], ld.at[3])

    def kv_load(s):
        return (pltpu.make_async_copy(k_hbm.at[s], kbuf.at[s], ld.at[4 + 2 * s]),
                pltpu.make_async_copy(v_hbm.at[s], vbuf.at[s], ld.at[5 + 2 * s]))

    for copy in small:
        copy.start()
    barrier = pltpu.get_barrier_semaphore()

    def greet(**axis):
        pl.semaphore_signal(barrier, inc=1, device_id=axis, device_id_type=MESH)

    loop(1, Z, lambda k: greet(ctx=p.ctx_of(p.z_at(k), y, c)))
    for k in range(1, Y):
        for cc in range(C):
            greet(ctx=p.ctx_of(z, p.y_at(k), cc))
    greet(ctx=p.ctx_of(z, y, 1 - c))
    def greet_tp(k):
        for cc in range(C):
            greet(ctx=p.ctx_of(z, y, cc), tp=p.tp_at(k))

    loop(1, T, greet_tp)
    for copy in [kv_load(s)[i] for i in (1, 0) for s in range(SEQS)]:
        copy.start()
    w_load.start()

    for copy in small:
        copy.wait()
    own = qin[...].astype(F32)
    for s in range(SEQS):
        for hd in range(HEADS):
            qrow[s * HEADS + hd:s * HEADS + hd + 1, :] = own[s:s + 1, hd * HD:(hd + 1) * HD]
    qbuf[y, c, z] = qrow[...].astype(BF16)
    qg = Gather(p, lambda yy: qbuf.at[yy, c], qsems)
    ag = Gather(p, lambda yy: abuf.at[yy], asems)
    pl.semaphore_wait(barrier, (Z - 1) + (Y * C - 1) + (T - 1) * C)
    qg.start()
    nk, nv = nkin[...].astype(F32), nvin[...].astype(F32)
    for s in range(SEQS):
        nkb[s] = jnp.broadcast_to(nk[s:s + 1], (PAD, HD)).astype(BF16)
        nvb[s] = jnp.broadcast_to(nv[s:s + 1], (8, HD))
    for pr in range(SEQS // 2):
        qd[pr] = jnp.zeros((2 * HD, 2 * rows), BF16)
        vt[pr, 2 * HD:, :] = jnp.ones((PAD, kbuf.shape[1]), BF16)

    def transpose(s):
        kv_load(s)[1].wait()
        at = pl.multiple_of(lax.rem(s, 2) * HD, HD)
        vt[s // 2, pl.ds(at, HD), :] = vbuf[s].T

    def attend(k):
        block = p.y_at(-k)
        x = qbuf[block].astype(F32).reshape(slots, SEQS, HEADS, HD)
        for s in range(SEQS):
            j = s % 2
            qd[s // 2, j * HD:(j + 1) * HD, j * rows:(j + 1) * rows] = x[:, s].reshape(rows, HD).T.astype(BF16)
        slot = lax.div(lax.rem(iota((8, 2 * rows), 1), rows), HEADS)
        token = lax.rem(slot, Z) * (Y * C) + block * C + lax.div(slot, Z)
        visible = token >= p.ctx
        chunk = min(CHUNK, kbuf.shape[1])
        chunks = [slice(a, a + chunk) for a in range(0, kbuf.shape[1], chunk)]

        def score(pr, at):
            keys = jnp.concatenate([kbuf[2 * pr, at], kbuf[2 * pr + 1, at]], axis=1)
            raw = jnp.dot(keys, qd[pr], preferred_element_type=F32)
            sbuf[pr, at] = raw
            return jnp.max(raw.reshape(chunk // 8, 8, 2 * rows), axis=0)

        def peak_of(pr, tops):
            keys = jnp.concatenate([nkb[2 * pr], nkb[2 * pr + 1]], axis=1)
            fresh = jnp.dot(keys, qd[pr], preferred_element_type=F32)[:8]
            fresh = jnp.where(visible, fresh, -jnp.inf)
            top = jnp.max(functools.reduce(jnp.maximum, tops + [fresh]), axis=0, keepdims=True)
            peak = rounded(top * SCALE)
            return peak, jnp.exp2(fresh * SCALE - peak)

        def weigh(pr, at, peak):
            pbuf[pr, at] = jnp.exp2(sbuf[pr, at] * SCALE - peak).astype(BF16)

        def finish(pr, peak, fresh):
            out = jnp.dot(vt[pr], pbuf[pr], preferred_element_type=F32)
            sub = iota((8, 2 * rows), 0)
            total = out[2 * HD:2 * HD + 8] + fresh
            three = jnp.where(sub == 0, peak, jnp.where(sub == 1, total, fresh))
            lane = iota((rows, HD), 1)
            row = iota((rows, HD), 0)
            for j in range(2):
                s = 2 * pr + j
                at = slice(j * rows, (j + 1) * rows)
                numer = out[j * HD:(j + 1) * HD, at].T
                cols = three[:, at].T
                numer = numer + rounded(cols[:, 2:3]) * nvb[s][:1]
                lead = rounded(cols[:, 1:2])
                rest = rounded(cols[:, 1:2] - lead)
                head = lax.rem(row, HEADS) + s * HEADS
                entry = jnp.where(lane == head, cols[:, 0:1], jnp.where(lane == head + 64, lead, jnp.where(lane == head + 96, rest, 0.0)))
                packed = jnp.sum(entry.reshape(slots, HEADS, HD), axis=1).reshape(C, Z, HD)
                st[k] = packed if s == 0 else st[k] + packed
                nb[k, :, :, s * HEADS:(s + 1) * HEADS, :] = numer.reshape(C, Z, HEADS, HD)

        tops = [score(0, at) for at in chunks]
        first = peak_of(0, tops)
        tops = []
        for at in chunks:
            tops.append(score(1, at))
            weigh(0, at, first[0])
        second = peak_of(1, tops)
        finish(0, *first)
        for at in chunks:
            weigh(1, at, second[0])
        finish(1, *second)

    def c_copy(k, group, send):
        block = qbuf.at[p.y_at(-k), c if send else 1 - c, qg.rows(group)]
        return p.copy(block, block, csems.at[0, group, k], csems.at[1, group, k], ctx=p.ctx_of(z, y, 1 - c))

    def w_copy():
        return p.copy(wbuf.at[c], wbuf.at[c], wsem.at[0], wsem.at[1], ctx=p.ctx_of(z, y, 1 - c))

    def core_at(j):
        return c if j == 0 else 1 - c

    def y_copy(k, j):
        dev = p.ctx_of(z, p.y_at(-k), core_at(j))
        return p.copy(ysb.at[k, j], yrb.at[k, j], ry.at[0, k, j], ry.at[1, k, j], ctx=dev)

    owners = Z // 2
    mine = z - Z // 4
    owner = (mine >= 0) & (mine < owners)

    def z_copies(o, index):
        dev = p.ctx_of(Z // 4 + o, y, c)
        at = pl.ds(2 * o, 2)
        return (p.copy(zsb.at[at], zrb.at[index], rz.at[0, 0, o], rz.at[1, 0, index], ctx=dev),
                p.copy(zss.at[at], zrs.at[index], rz.at[0, 1, o], rz.at[1, 1, index], ctx=dev))

    def others(last, here, body):
        def one(i):
            @pl.when(i != here)
            def _():
                body(i)
        loop(0, last, one)

    def a_copy(to, o):
        block = abuf.at[y, pl.ds(2 * o, 2)]
        return p.copy(block, block, az.at[0, to], az.at[1, o], ctx=p.ctx_of(to, y, c))

    def t_copy(k, j):
        to = p.tp_at(k)
        return p.copy(ts.at[to * C + core_at(j)], tr.at[k * C + j], tt.at[0], tt.at[1], ctx=p.ctx_of(z, y, core_at(j)), tp=to)

    def t_all():
        block = tr.at[pl.ds(1, T * C - 1)]
        return p.copy(block, block, tt.at[0], tt.at[1], ctx=p.ctx_of(z, y, 1 - c))

    def message(stats, numer):
        pad = jnp.concatenate([stats, jnp.zeros((PAD - Z, HD), F32)], axis=0)
        return jnp.concatenate([numer.reshape(Z * UNIT, HD), pad], axis=0).astype(BF16)

    def reduce_y(k):
        ysb[k, 1] = message(st[k, 1 - c], nb[k, 1 - c])
        y_copy(k, 1).start()

        @pl.when(k > 0)
        def _():
            ysb[k, 0] = message(st[k, c], nb[k, c])
            y_copy(k, 0).start()

    def received(k, j):
        y_copy(k, j).wait_recv()
        got = yrb[k, j].astype(F32)
        return got[Z * UNIT:Z * UNIT + Z], got[:Z * UNIT].reshape(Z, UNIT, HD)

    def reduce_z():
        early = [(st[0, c], nb[0, c]), received(0, 1)] + [received(k, j) for k in units[:-1] for j in range(C)]
        peak, total, numer = merge(*zip(*early))
        late = [(pack(peak, total), numer)] + [received(units[-1], j) for j in range(C)]
        peak, total, numer = merge(*zip(*late))
        stats = pack(peak, total)
        zsb[...] = numer.astype(BF16)
        for k in range(Z):
            zss[k] = stats[k:k + 1]

        def send(o):
            for copy in z_copies(o, z):
                copy.start()
        others(owners, mine, send)

    def attended():
        at = pl.ds(2 * mine, 2)
        zrb[z] = zsb[at]
        zrs[z] = zss[at]

        def wait(i):
            for copy in z_copies(mine, i):
                copy.wait_recv()
        others(Z, z, wait)
        stats = [jnp.concatenate([zrs[i, 0], zrs[i, 1]], axis=0) for i in range(Z)]
        peak, total, numer = merge(stats, [zrb[i].astype(F32) for i in range(Z)])
        abuf[y, at] = (numer / spread(total, 64)).astype(BF16)
        others(Z, z, lambda to: a_copy(to, mine).start())

    def project(group):
        for k in near:
            ag.y_copy(k, group, False).wait_recv()
        H = Z // 2
        n = Y * H * SEQS
        af[...] = abuf[:, ag.rows(group)].reshape(n * HEADS, HD).astype(F32)
        heads = [af[pl.ds(hd, n, stride=HEADS), :].astype(BF16) for hd in range(HEADS)]
        both = jnp.dot(jnp.concatenate(heads, axis=1), jnp.concatenate([wbuf[0], wbuf[1]], axis=1), preferred_element_type=F32)
        for cc in range(C):
            pf[group, cc] = both[:, cc * HD:(cc + 1) * HD]
        for zz in range(H):
            t = ag.half_at(group) * H + zz
            for cc in range(C):
                tile = [pf[group, cc, pl.ds(SEQS * zz + s, Y, stride=SEQS * H), :] for s in range(SEQS)]
                tile = jnp.concatenate(tile, axis=0)
                tf[t * C + cc] = tile
                ts[t * C + cc] = tile.astype(BF16)

        def send(zz):
            k = lax.rem(ag.half_at(group) * H + zz - p.tp + T, T)

            @pl.when(k > 0)
            def _():
                t_copy(k, 0).start()
            t_copy(k, 1).start()
        loop(0, H, send)

    loop(0, SEQS // 2, transpose)
    for group in range(2):
        qg.z_arrived(group)
        c_copy(0, group, True).start()
        qg.along_y(group, units)
    w_load.wait()
    w_copy().start()
    loop(SEQS // 2, SEQS, transpose)
    loop(0, SEQS, lambda s: kv_load(s)[0].wait())

    def unit(i):
        k = unit_at(i)
        for group in range(2):
            c_copy(k, group, False).wait_recv()
        attend(k)
        reduce_y(k)

        @pl.when(i == 0)
        def _():
            for k in near:
                qg.arrived(k)
                for group in range(2):
                    c_copy(k, group, True).start()

    loop(0, Y, unit)
    reduce_z()
    pl.when(owner)(attended)
    w_copy().wait_recv()
    for group in range(2):
        for o in range(owners // 2):
            at = ag.half_at(group) * (owners // 2) + o

            @pl.when(at != mine)
            def _():
                a_copy(z, at).wait_recv()
        ag.along_y(group, units)
    for group in range(2):
        project(group)
    same = tf[p.tp * C + c]
    t_all().wait_recv()
    for k in range(1, T):
        same = same + tr[k * C].astype(F32)
    other = sum(tr[k * C + 1].astype(F32) for k in range(T))
    for s in range(SEQS):
        of[pl.ds(s * Y * C + c, Y, stride=C), :] = same[s * Y:(s + 1) * Y]
        of[pl.ds(s * Y * C + 1 - c, Y, stride=C), :] = other[s * Y:(s + 1) * Y]
    o_ref[...] = of[...].astype(BF16)

    qg.drain(True)
    ag.drain(False)
    w_copy().wait_send()
    for k in range(Y):
        for group in range(2):
            c_copy(k, group, True).wait_send()
        for j in range(C):
            if k + j:
                y_copy(k, j).wait_send()

    def sent(o):
        for copy in z_copies(o, z):
            copy.wait_send()
    others(owners, mine, sent)

    @pl.when(owner)
    def _():
        others(Z, z, lambda to: a_copy(to, mine).wait_send())

    t_all().wait_send()


def build(sizes, queries, keys, values, new_keys, new_values, weight):
    Z, Y, C, T = sizes
    S = keys.shape[1]
    V = pltpu.VMEM
    dma = pltpu.SemaphoreType.DMA
    slots = C * Z
    rows = slots * HEADS
    out_rows = SEQS * Y * C
    block = Z * UNIT + PAD
    tile = SEQS * Y
    scratch = [
        V((SEQS, S, HD), BF16), V((SEQS, S, HD), BF16), V((SEQS // 2, 2 * HD + PAD, S), BF16), V((C,) + weight.shape, BF16),
        V((SEQS, HEADS * HD), BF16), V((SEQS, HD), BF16), V((SEQS, HD), BF16),
        V((SEQS, PAD, HD), BF16), V((SEQS, 8, HD), F32), V((UNIT, HD), F32),
        V((Y, C, Z, UNIT, HD), BF16), V((SEQS // 2, 2 * HD, 2 * rows), BF16),
        V((SEQS // 2, S, 2 * rows), F32), V((SEQS // 2, S, 2 * rows), BF16),
        V((Y, C, Z, UNIT, HD), F32), V((Y, C, Z, HD), F32),
        V((Y, C, block, HD), BF16), V((Y, C, block, HD), BF16),
        V((Z, UNIT, HD), BF16), V((Z, 1, HD), F32),
        V((Z, 2, UNIT, HD), BF16), V((Z, 2, 1, HD), F32),
        V((Y, Z, UNIT, HD), BF16), V((Y * Z // 2 * UNIT, HD), F32), V((2, C, Y * Z // 2 * SEQS, HD), F32),
        V((T * C, tile, HD), F32), V((T * C, tile, HD), BF16), V((T * C, tile, HD), BF16), V((out_rows, HD), F32),
        dma((4 + 2 * SEQS,)), [dma((2, 2)), dma((2, Y - 1)), dma((2, Y - 1))], dma((2, 2, Y)),
        [dma((2, 2)), dma((2, Y - 1)), dma((2, Y - 1))], dma((2,)), dma((2, Y, C)),
        dma((2, 2, Z)), dma((2, Z)), dma((2,)),
    ]
    out = pl.pallas_call(
        functools.partial(kernel, sizes),
        out_shape=jax.ShapeDtypeStruct((out_rows, HD), BF16),
        in_specs=[pl.BlockSpec(memory_space=pltpu.HBM)] * 6,
        out_specs=pl.BlockSpec(memory_space=pltpu.VMEM),
        scratch_shapes=scratch,
        compiler_params=pltpu.CompilerParams(
            collective_id=0, has_side_effects=True, vmem_limit_bytes=64 * 1024 * 1024
        ),
        cost_estimate=pl.CostEstimate(
            flops=4 * SEQS * Y * rows * S * HD, bytes_accessed=4 * SEQS * S * HD,
            transcendentals=SEQS * Y * rows * S,
        ),
    )(
        queries.reshape(SEQS, HEADS * HD), keys, values,
        new_keys.reshape(SEQS, HD), new_values.reshape(SEQS, HD), weight,
    )
    return out.reshape(SEQS, Y * C, HD)


def solution(mesh):
    Z = mesh.shape["tp"]
    sizes = (Z, mesh.shape["ctx"] // (2 * Z), 2, mesh.shape["tp"])
    spec = P(None, "ctx", "tp")
    return jax.shard_map(
        functools.partial(build, sizes),
        mesh=mesh,
        in_specs=(spec, spec, spec, spec, spec, P("tp", "ctx")),
        out_specs=P(None, "tp", "ctx"),
        check_vma=False,
    )
```

```python
import functools
import math

import jax
import jax.numpy as jnp
from jax import lax
from jax.experimental import pallas as pl
from jax.experimental.pallas import tpu as pltpu
from jax.sharding import PartitionSpec as P

HD = 128
HEADS = 8
SEQS = 4
UNIT = SEQS * HEADS
PAD = 16
CHUNK = 128
SCALE = math.log2(math.e) / math.sqrt(HD)
MESH = pl.DeviceIdType.MESH
F32 = jnp.float32
BF16 = jnp.bfloat16


def iota(shape, dim):
    return lax.broadcasted_iota(jnp.int32, shape, dim)


def loop(first, last, body):
    lax.fori_loop(first, last, lambda i, c: (body(i), c)[1], 0)


def rounded(x):
    return x.astype(BF16).astype(F32)


def spread(packed, first):
    shape = (packed.shape[0], UNIT, HD)
    wide = jnp.broadcast_to(packed[:, None, :], shape)
    hit = iota(shape, 2) == iota(shape, 1) + first
    return jnp.sum(jnp.where(hit, wide, 0.0), axis=-1, keepdims=True)


def merge(stats, numers):
    peak = functools.reduce(jnp.maximum, stats)
    factors = [jnp.exp2(s - peak) for s in stats]
    total = sum((s + pltpu.roll(s, 96, 1)) * pltpu.roll(f, 64, 1) for s, f in zip(stats, factors))
    out = sum(n * spread(f, 0) for n, f in zip(numers, factors))
    return peak, total, out


def pack(peak, total):
    lead = rounded(total)
    rest = rounded(total - lead)
    lane = iota(peak.shape, 1)
    return jnp.where(lane < 64, peak, jnp.where(lane < 96, lead, pltpu.roll(rest, 32, 1)))


class Place:
    def __init__(self, sizes):
        self.Z, self.Y, self.C, self.T = sizes
        ctx = lax.axis_index("ctx")
        self.c = lax.rem(ctx, self.C)
        self.y = lax.rem(ctx // self.C, self.Y)
        self.z = ctx // (self.C * self.Y)
        self.ctx = ctx
        self.tp = lax.axis_index("tp")

    def z_at(self, k):
        return lax.rem(self.z + k + self.Z, self.Z)

    def y_at(self, k):
        return lax.rem(self.y + k + self.Y, self.Y)

    def tp_at(self, k):
        return lax.rem(self.tp + k + self.T, self.T)

    def ctx_of(self, z, y, c):
        return (z * self.Y + y) * self.C + c

    def copy(self, src, dst, send, recv, **axis):
        return pltpu.make_async_remote_copy(
            src_ref=src, dst_ref=dst, send_sem=send, recv_sem=recv, device_id=axis, device_id_type=MESH
        )


class Gather:
    def __init__(self, place, part, sems):
        self.p, self.part, self.H = place, part, place.Z // 2
        self.zz, self.ys, self.yr = sems
        self.half = place.z // self.H

    def z_copy(self, to, group):
        p = self.p
        block = self.part(p.y).at[p.z]
        return p.copy(block, block, self.zz.at[0, group], self.zz.at[1, group], ctx=p.ctx_of(to, p.y, p.c))

    def z_all(self, group):
        p = self.p
        block = self.part(p.y).at[pl.ds(0, self.H - 1 + group)]
        return p.copy(block, block, self.zz.at[0, group], self.zz.at[1, group], ctx=p.ctx_of(p.z_at(1), p.y, p.c))

    def half_at(self, group):
        return self.half if group == 0 else 1 - self.half

    def rows(self, group):
        return pl.ds(self.half_at(group) * self.H, self.H)

    def y_copy(self, k, group, send):
        p = self.p
        block = self.part(p.y if send else p.y_at(-k)).at[self.rows(group)]
        return p.copy(block, block, self.ys.at[group, k - 1], self.yr.at[group, k - 1], ctx=p.ctx_of(p.z, p.y_at(k), p.c))

    def start(self):
        H = self.H
        loop(0, H, lambda j: self.z_copy((1 - self.half) * H + lax.rem(self.p.z + j, H), 1).start())
        loop(1, H, lambda j: self.z_copy(self.half * H + lax.rem(self.p.z + j, H), 0).start())

    def z_arrived(self, group):
        if self.H - 1 + group:
            self.z_all(group).wait_recv()

    def along_y(self, group, order):
        for k in order:
            self.y_copy(k, group, True).start()

    def arrived(self, k):
        for group in range(2):
            self.y_copy(k, group, False).wait_recv()

    def drain(self, z_too):
        for group in range(2):
            if z_too and self.H - 1 + group:
                self.z_all(group).wait_send()
            for k in range(1, self.p.Y):
                self.y_copy(k, group, True).wait_send()


def kernel(sizes, q_hbm, k_hbm, v_hbm, nk_hbm, nv_hbm, w_hbm, o_ref,
           kbuf, vbuf, vt, wbuf, qin, nkin, nvin, nkb, nvb, qrow, qbuf, qd, sbuf, pbuf, nb, st,
           ysb, yrb, zsb, zss, zrb, zrs, abuf, af, pf, tf, ts, tr, of,
           ld, qsems, csems, asems, wsem, ry, rz, az, tt):
    p = Place(sizes)
    Z, Y, C, T = sizes
    z, y, c = p.z, p.y, p.c
    slots = C * Z
    rows = slots * HEADS
    near = [k for k in (1, 3, 2) if k < Y]
    units = [k for k in (2, 1, 3) if k < Y]

    def unit_at(i):
        return lax.rem(i, 2) * 2 + i // 2 if Y == 4 else i

    small = [pltpu.make_async_copy(a, b, ld.at[i]) for i, (a, b) in enumerate(((q_hbm, qin), (nk_hbm, nkin), (nv_hbm, nvin)))]
    w_load = pltpu.make_async_copy(w_hbm, wbuf.at[c], ld.at[3])

    def kv_load(s):
        return (pltpu.make_async_copy(k_hbm.at[s], kbuf.at[s], ld.at[4 + 2 * s]),
                pltpu.make_async_copy(v_hbm.at[s], vbuf.at[s], ld.at[5 + 2 * s]))

    for copy in small:
        copy.start()
    barrier = pltpu.get_barrier_semaphore()

    def greet(**axis):
        pl.semaphore_signal(barrier, inc=1, device_id=axis, device_id_type=MESH)

    loop(1, Z, lambda k: greet(ctx=p.ctx_of(p.z_at(k), y, c)))
    for k in range(1, Y):
        for cc in range(C):
            greet(ctx=p.ctx_of(z, p.y_at(k), cc))
    greet(ctx=p.ctx_of(z, y, 1 - c))
    def greet_tp(k):
        for cc in range(C):
            greet(ctx=p.ctx_of(z, y, cc), tp=p.tp_at(k))

    loop(1, T, greet_tp)
    for copy in [kv_load(s)[i] for i in (1, 0) for s in range(SEQS)]:
        copy.start()
    w_load.start()

    for copy in small:
        copy.wait()
    own = qin[...].astype(F32)
    for s in range(SEQS):
        for hd in range(HEADS):
            qrow[s * HEADS + hd:s * HEADS + hd + 1, :] = own[s:s + 1, hd * HD:(hd + 1) * HD]
    qbuf[y, c, z] = qrow[...].astype(BF16)
    qg = Gather(p, lambda yy: qbuf.at[yy, c], qsems)
    ag = Gather(p, lambda yy: abuf.at[yy], asems)
    pl.semaphore_wait(barrier, (Z - 1) + (Y * C - 1) + (T - 1) * C)
    qg.start()
    nk, nv = nkin[...].astype(F32), nvin[...].astype(F32)
    for s in range(SEQS):
        nkb[s] = jnp.broadcast_to(nk[s:s + 1], (PAD, HD)).astype(BF16)
        nvb[s] = jnp.broadcast_to(nv[s:s + 1], (8, HD))
    for pr in range(SEQS // 2):
        qd[pr] = jnp.zeros((2 * HD, 2 * rows), BF16)
        vt[pr, 2 * HD:, :] = jnp.ones((PAD, kbuf.shape[1]), BF16)

    def transpose(s):
        kv_load(s)[1].wait()
        at = pl.multiple_of(lax.rem(s, 2) * HD, HD)
        vt[s // 2, pl.ds(at, HD), :] = vbuf[s].T

    def attend(k):
        block = p.y_at(-k)
        x = qbuf[block].astype(F32).reshape(slots, SEQS, HEADS, HD)
        for s in range(SEQS):
            j = s % 2
            qd[s // 2, j * HD:(j + 1) * HD, j * rows:(j + 1) * rows] = x[:, s].reshape(rows, HD).T.astype(BF16)
        slot = lax.div(lax.rem(iota((8, 2 * rows), 1), rows), HEADS)
        token = lax.rem(slot, Z) * (Y * C) + block * C + lax.div(slot, Z)
        visible = token >= p.ctx
        chunk = min(CHUNK, kbuf.shape[1])
        chunks = [slice(a, a + chunk) for a in range(0, kbuf.shape[1], chunk)]

        def score(pr, at):
            keys = jnp.concatenate([kbuf[2 * pr, at], kbuf[2 * pr + 1, at]], axis=1)
            raw = jnp.dot(keys, qd[pr], preferred_element_type=F32)
            sbuf[pr, at] = raw
            return jnp.max(raw.reshape(chunk // 8, 8, 2 * rows), axis=0)

        def peak_of(pr, tops):
            keys = jnp.concatenate([nkb[2 * pr], nkb[2 * pr + 1]], axis=1)
            fresh = jnp.dot(keys, qd[pr], preferred_element_type=F32)[:8]
            fresh = jnp.where(visible, fresh, -jnp.inf)
            top = jnp.max(functools.reduce(jnp.maximum, tops + [fresh]), axis=0, keepdims=True)
            peak = rounded(top * SCALE)
            return peak, jnp.exp2(fresh * SCALE - peak)

        def weigh(pr, at, peak):
            pbuf[pr, at] = jnp.exp2(sbuf[pr, at] * SCALE - peak).astype(BF16)

        def finish(pr, peak, fresh):
            out = jnp.dot(vt[pr], pbuf[pr], preferred_element_type=F32)
            sub = iota((8, 2 * rows), 0)
            total = out[2 * HD:2 * HD + 8] + fresh
            three = jnp.where(sub == 0, peak, jnp.where(sub == 1, total, fresh))
            lane = iota((rows, HD), 1)
            row = iota((rows, HD), 0)
            for j in range(2):
                s = 2 * pr + j
                at = slice(j * rows, (j + 1) * rows)
                numer = out[j * HD:(j + 1) * HD, at].T
                cols = three[:, at].T
                numer = numer + rounded(cols[:, 2:3]) * nvb[s][:1]
                lead = rounded(cols[:, 1:2])
                rest = rounded(cols[:, 1:2] - lead)
                head = lax.rem(row, HEADS) + s * HEADS
                entry = jnp.where(lane == head, cols[:, 0:1], jnp.where(lane == head + 64, lead, jnp.where(lane == head + 96, rest, 0.0)))
                packed = jnp.sum(entry.reshape(slots, HEADS, HD), axis=1).reshape(C, Z, HD)
                st[k] = packed if s == 0 else st[k] + packed
                nb[k, :, :, s * HEADS:(s + 1) * HEADS, :] = numer.reshape(C, Z, HEADS, HD)

        tops = [score(0, at) for at in chunks]
        first = peak_of(0, tops)
        tops = []
        for at in chunks:
            tops.append(score(1, at))
            weigh(0, at, first[0])
        second = peak_of(1, tops)
        finish(0, *first)
        for at in chunks:
            weigh(1, at, second[0])
        finish(1, *second)

    def c_copy(k, group, send):
        block = qbuf.at[p.y_at(-k), c if send else 1 - c, qg.rows(group)]
        return p.copy(block, block, csems.at[0, group, k], csems.at[1, group, k], ctx=p.ctx_of(z, y, 1 - c))

    def w_copy():
        return p.copy(wbuf.at[c], wbuf.at[c], wsem.at[0], wsem.at[1], ctx=p.ctx_of(z, y, 1 - c))

    def core_at(j):
        return c if j == 0 else 1 - c

    def y_copy(k, j):
        dev = p.ctx_of(z, p.y_at(-k), core_at(j))
        return p.copy(ysb.at[k, j], yrb.at[k, j], ry.at[0, k, j], ry.at[1, k, j], ctx=dev)

    owners = Z // 2
    mine = z - Z // 4
    owner = (mine >= 0) & (mine < owners)

    def z_copies(o, index):
        dev = p.ctx_of(Z // 4 + o, y, c)
        at = pl.ds(2 * o, 2)
        return (p.copy(zsb.at[at], zrb.at[index], rz.at[0, 0, o], rz.at[1, 0, index], ctx=dev),
                p.copy(zss.at[at], zrs.at[index], rz.at[0, 1, o], rz.at[1, 1, index], ctx=dev))

    def others(last, here, body):
        def one(i):
            @pl.when(i != here)
            def _():
                body(i)
        loop(0, last, one)

    def a_copy(to, o):
        block = abuf.at[y, pl.ds(2 * o, 2)]
        return p.copy(block, block, az.at[0, to], az.at[1, o], ctx=p.ctx_of(to, y, c))

    def t_copy(k, j):
        to = p.tp_at(k)
        return p.copy(ts.at[to * C + core_at(j)], tr.at[k * C + j], tt.at[0], tt.at[1], ctx=p.ctx_of(z, y, core_at(j)), tp=to)

    def t_all():
        block = tr.at[pl.ds(1, T * C - 1)]
        return p.copy(block, block, tt.at[0], tt.at[1], ctx=p.ctx_of(z, y, 1 - c))

    def message(stats, numer):
        pad = jnp.concatenate([stats, jnp.zeros((PAD - Z, HD), F32)], axis=0)
        return jnp.concatenate([numer.reshape(Z * UNIT, HD), pad], axis=0).astype(BF16)

    def reduce_y(k):
        ysb[k, 1] = message(st[k, 1 - c], nb[k, 1 - c])
        y_copy(k, 1).start()

        @pl.when(k > 0)
        def _():
            ysb[k, 0] = message(st[k, c], nb[k, c])
            y_copy(k, 0).start()

    def received(k, j):
        y_copy(k, j).wait_recv()
        got = yrb[k, j].astype(F32)
        return got[Z * UNIT:Z * UNIT + Z], got[:Z * UNIT].reshape(Z, UNIT, HD)

    def reduce_z():
        early = [(st[0, c], nb[0, c]), received(0, 1)] + [received(k, j) for k in units[:-1] for j in range(C)]
        peak, total, numer = merge(*zip(*early))
        late = [(pack(peak, total), numer)] + [received(units[-1], j) for j in range(C)]
        peak, total, numer = merge(*zip(*late))
        stats = pack(peak, total)
        zsb[...] = numer.astype(BF16)
        for k in range(Z):
            zss[k] = stats[k:k + 1]

        def send(o):
            for copy in z_copies(o, z):
                copy.start()
        others(owners, mine, send)

    def attended():
        at = pl.ds(2 * mine, 2)
        zrb[z] = zsb[at]
        zrs[z] = zss[at]

        def wait(i):
            for copy in z_copies(mine, i):
                copy.wait_recv()
        others(Z, z, wait)
        stats = [jnp.concatenate([zrs[i, 0], zrs[i, 1]], axis=0) for i in range(Z)]
        peak, total, numer = merge(stats, [zrb[i].astype(F32) for i in range(Z)])
        abuf[y, at] = (numer / spread(total, 64)).astype(BF16)
        others(Z, z, lambda to: a_copy(to, mine).start())

    def project(group):
        for k in near:
            ag.y_copy(k, group, False).wait_recv()
        H = Z // 2
        n = Y * H * SEQS
        af[...] = abuf[:, ag.rows(group)].reshape(n * HEADS, HD).astype(F32)
        heads = [af[pl.ds(hd, n, stride=HEADS), :].astype(BF16) for hd in range(HEADS)]
        both = jnp.dot(jnp.concatenate(heads, axis=1), jnp.concatenate([wbuf[0], wbuf[1]], axis=1), preferred_element_type=F32)
        for cc in range(C):
            pf[group, cc] = both[:, cc * HD:(cc + 1) * HD]
        for zz in range(H):
            t = ag.half_at(group) * H + zz
            for cc in range(C):
                tile = [pf[group, cc, pl.ds(SEQS * zz + s, Y, stride=SEQS * H), :] for s in range(SEQS)]
                tile = jnp.concatenate(tile, axis=0)
                tf[t * C + cc] = tile
                ts[t * C + cc] = tile.astype(BF16)

        def send(zz):
            k = lax.rem(ag.half_at(group) * H + zz - p.tp + T, T)

            @pl.when(k > 0)
            def _():
                t_copy(k, 0).start()
            t_copy(k, 1).start()
        loop(0, H, send)

    loop(0, SEQS // 2, transpose)
    for group in range(2):
        qg.z_arrived(group)
        c_copy(0, group, True).start()
        qg.along_y(group, units)
    w_load.wait()
    w_copy().start()
    loop(SEQS // 2, SEQS, transpose)
    loop(0, SEQS, lambda s: kv_load(s)[0].wait())

    def unit(i):
        k = unit_at(i)
        for group in range(2):
            c_copy(k, group, False).wait_recv()
        attend(k)
        reduce_y(k)

        @pl.when(i == 0)
        def _():
            for k in near:
                qg.arrived(k)
                for group in range(2):
                    c_copy(k, group, True).start()

    loop(0, Y, unit)
    reduce_z()
    pl.when(owner)(attended)
    w_copy().wait_recv()
    for group in range(2):
        for o in range(owners // 2):
            at = ag.half_at(group) * (owners // 2) + o

            @pl.when(at != mine)
            def _():
                a_copy(z, at).wait_recv()
        ag.along_y(group, units)
    for group in range(2):
        project(group)
    same = tf[p.tp * C + c]
    t_all().wait_recv()
    for k in range(1, T):
        same = same + tr[k * C].astype(F32)
    other = sum(tr[k * C + 1].astype(F32) for k in range(T))
    for s in range(SEQS):
        of[pl.ds(s * Y * C + c, Y, stride=C), :] = same[s * Y:(s + 1) * Y]
        of[pl.ds(s * Y * C + 1 - c, Y, stride=C), :] = other[s * Y:(s + 1) * Y]
    o_ref[...] = of[...].astype(BF16)

    qg.drain(True)
    ag.drain(False)
    w_copy().wait_send()
    for k in range(Y):
        for group in range(2):
            c_copy(k, group, True).wait_send()
        for j in range(C):
            if k + j:
                y_copy(k, j).wait_send()

    def sent(o):
        for copy in z_copies(o, z):
            copy.wait_send()
    others(owners, mine, sent)

    @pl.when(owner)
    def _():
        others(Z, z, lambda to: a_copy(to, mine).wait_send())

    t_all().wait_send()


def build(sizes, queries, keys, values, new_keys, new_values, weight):
    Z, Y, C, T = sizes
    S = keys.shape[1]
    V = pltpu.VMEM
    dma = pltpu.SemaphoreType.DMA
    slots = C * Z
    rows = slots * HEADS
    out_rows = SEQS * Y * C
    block = Z * UNIT + PAD
    tile = SEQS * Y
    scratch = [
        V((SEQS, S, HD), BF16), V((SEQS, S, HD), BF16), V((SEQS // 2, 2 * HD + PAD, S), BF16), V((C,) + weight.shape, BF16),
        V((SEQS, HEADS * HD), BF16), V((SEQS, HD), BF16), V((SEQS, HD), BF16),
        V((SEQS, PAD, HD), BF16), V((SEQS, 8, HD), F32), V((UNIT, HD), F32),
        V((Y, C, Z, UNIT, HD), BF16), V((SEQS // 2, 2 * HD, 2 * rows), BF16),
        V((SEQS // 2, S, 2 * rows), F32), V((SEQS // 2, S, 2 * rows), BF16),
        V((Y, C, Z, UNIT, HD), F32), V((Y, C, Z, HD), F32),
        V((Y, C, block, HD), BF16), V((Y, C, block, HD), BF16),
        V((Z, UNIT, HD), BF16), V((Z, 1, HD), F32),
        V((Z, 2, UNIT, HD), BF16), V((Z, 2, 1, HD), F32),
        V((Y, Z, UNIT, HD), BF16), V((Y * Z // 2 * UNIT, HD), F32), V((2, C, Y * Z // 2 * SEQS, HD), F32),
        V((T * C, tile, HD), F32), V((T * C, tile, HD), BF16), V((T * C, tile, HD), BF16), V((out_rows, HD), F32),
        dma((4 + 2 * SEQS,)), [dma((2, 2)), dma((2, Y - 1)), dma((2, Y - 1))], dma((2, 2, Y)),
        [dma((2, 2)), dma((2, Y - 1)), dma((2, Y - 1))], dma((2,)), dma((2, Y, C)),
        dma((2, 2, Z)), dma((2, Z)), dma((2,)),
    ]
    out = pl.pallas_call(
        functools.partial(kernel, sizes),
        out_shape=jax.ShapeDtypeStruct((out_rows, HD), BF16),
        in_specs=[pl.BlockSpec(memory_space=pltpu.HBM)] * 6,
        out_specs=pl.BlockSpec(memory_space=pltpu.VMEM),
        scratch_shapes=scratch,
        compiler_params=pltpu.CompilerParams(
            collective_id=0, has_side_effects=True, vmem_limit_bytes=64 * 1024 * 1024
        ),
        cost_estimate=pl.CostEstimate(
            flops=4 * SEQS * Y * rows * S * HD, bytes_accessed=4 * SEQS * S * HD,
            transcendentals=SEQS * Y * rows * S,
        ),
    )(
        queries.reshape(SEQS, HEADS * HD), keys, values,
        new_keys.reshape(SEQS, HD), new_values.reshape(SEQS, HD), weight,
    )
    return out.reshape(SEQS, Y * C, HD)


def solution(mesh):
    Z = mesh.shape["tp"]
    sizes = (Z, mesh.shape["ctx"] // (2 * Z), 2, mesh.shape["tp"])
    spec = P(None, "ctx", "tp")
    return jax.shard_map(
        functools.partial(build, sizes),
        mesh=mesh,
        in_specs=(spec, spec, spec, spec, spec, P("tp", "ctx")),
        out_specs=P(None, "tp", "ctx"),
        check_vma=False,
    )
```

```python
import functools
import math

import jax
import jax.numpy as jnp
from jax import lax
from jax.experimental import pallas as pl
from jax.experimental.pallas import tpu as pltpu
from jax.sharding import PartitionSpec as P

HD = 128
HEADS = 8
SEQS = 4
UNIT = SEQS * HEADS
PAD = 16
CHUNK = 256
SCALE = math.log2(math.e) / math.sqrt(HD)
MESH = pl.DeviceIdType.MESH
F32 = jnp.float32
BF16 = jnp.bfloat16


def iota(shape, dim):
    return lax.broadcasted_iota(jnp.int32, shape, dim)


def loop(first, last, body):
    lax.fori_loop(first, last, lambda i, c: (body(i), c)[1], 0)


def rounded(x):
    return x.astype(BF16).astype(F32)


def spread(packed, first):
    shape = (packed.shape[0], UNIT, HD)
    wide = jnp.broadcast_to(packed[:, None, :], shape)
    hit = iota(shape, 2) == iota(shape, 1) + first
    return jnp.sum(jnp.where(hit, wide, 0.0), axis=-1, keepdims=True)


def merge(stats, numers):
    peak = functools.reduce(jnp.maximum, stats)
    factors = [jnp.exp2(s - peak) for s in stats]
    total = sum((s + pltpu.roll(s, 96, 1)) * pltpu.roll(f, 64, 1) for s, f in zip(stats, factors))
    out = sum(n * spread(f, 0) for n, f in zip(numers, factors))
    return peak, total, out


def pack(peak, total):
    lead = rounded(total)
    rest = rounded(total - lead)
    lane = iota(peak.shape, 1)
    return jnp.where(lane < 64, peak, jnp.where(lane < 96, lead, pltpu.roll(rest, 32, 1)))


class Place:
    def __init__(self, sizes):
        self.Z, self.Y, self.C, self.T = sizes
        ctx = lax.axis_index("ctx")
        self.c = lax.rem(ctx, self.C)
        self.y = lax.rem(ctx // self.C, self.Y)
        self.z = ctx // (self.C * self.Y)
        self.ctx = ctx
        self.tp = lax.axis_index("tp")

    def z_at(self, k):
        return lax.rem(self.z + k + self.Z, self.Z)

    def y_at(self, k):
        return lax.rem(self.y + k + self.Y, self.Y)

    def tp_at(self, k):
        return lax.rem(self.tp + k + self.T, self.T)

    def ctx_of(self, z, y, c):
        return (z * self.Y + y) * self.C + c

    def copy(self, src, dst, send, recv, **axis):
        return pltpu.make_async_remote_copy(
            src_ref=src, dst_ref=dst, send_sem=send, recv_sem=recv, device_id=axis, device_id_type=MESH
        )


class Gather:
    def __init__(self, place, part, sems):
        self.p, self.part, self.H = place, part, place.Z // 2
        self.zz, self.ys, self.yr = sems
        self.half = place.z // self.H

    def z_copy(self, to, group):
        p = self.p
        block = self.part(p.y).at[p.z]
        return p.copy(block, block, self.zz.at[0, group], self.zz.at[1, group], ctx=p.ctx_of(to, p.y, p.c))

    def z_all(self, group):
        p = self.p
        block = self.part(p.y).at[pl.ds(0, self.H - 1 + group)]
        return p.copy(block, block, self.zz.at[0, group], self.zz.at[1, group], ctx=p.ctx_of(p.z_at(1), p.y, p.c))

    def half_at(self, group):
        return self.half if group == 0 else 1 - self.half

    def rows(self, group):
        return pl.ds(self.half_at(group) * self.H, self.H)

    def y_copy(self, k, group, send):
        p = self.p
        block = self.part(p.y if send else p.y_at(-k)).at[self.rows(group)]
        return p.copy(block, block, self.ys.at[group, k - 1], self.yr.at[group, k - 1], ctx=p.ctx_of(p.z, p.y_at(k), p.c))

    def start(self):
        H = self.H
        loop(0, H, lambda j: self.z_copy((1 - self.half) * H + lax.rem(self.p.z + j, H), 1).start())
        loop(1, H, lambda j: self.z_copy(self.half * H + lax.rem(self.p.z + j, H), 0).start())

    def z_arrived(self, group):
        if self.H - 1 + group:
            self.z_all(group).wait_recv()

    def along_y(self, group, order):
        for k in order:
            self.y_copy(k, group, True).start()

    def arrived(self, k):
        for group in range(2):
            self.y_copy(k, group, False).wait_recv()

    def drain(self, z_too):
        for group in range(2):
            if z_too and self.H - 1 + group:
                self.z_all(group).wait_send()
            for k in range(1, self.p.Y):
                self.y_copy(k, group, True).wait_send()


def kernel(sizes, q_hbm, k_hbm, v_hbm, nk_hbm, nv_hbm, w_hbm, o_ref,
           kbuf, vbuf, vt, wbuf, qin, nkin, nvin, nkb, nvb, qrow, qbuf, qd, sbuf, pbuf, nb, st,
           ysb, yrb, zsb, zss, zrb, zrs, abuf, af, pf, tf, ts, tr, of,
           ld, qsems, csems, asems, wsem, ry, rz, az, tt):
    p = Place(sizes)
    Z, Y, C, T = sizes
    z, y, c = p.z, p.y, p.c
    slots = C * Z
    rows = slots * HEADS
    near = [k for k in (1, 3, 2) if k < Y]
    units = [k for k in (2, 1, 3) if k < Y]

    def unit_at(i):
        return lax.rem(i, 2) * 2 + i // 2 if Y == 4 else i

    small = [pltpu.make_async_copy(a, b, ld.at[i]) for i, (a, b) in enumerate(((q_hbm, qin), (nk_hbm, nkin), (nv_hbm, nvin)))]
    w_load = pltpu.make_async_copy(w_hbm, wbuf.at[c], ld.at[3])

    def kv_load(s):
        return (pltpu.make_async_copy(k_hbm.at[s], kbuf.at[s], ld.at[4 + 2 * s]),
                pltpu.make_async_copy(v_hbm.at[s], vbuf.at[s], ld.at[5 + 2 * s]))

    for copy in small:
        copy.start()
    barrier = pltpu.get_barrier_semaphore()

    def greet(**axis):
        pl.semaphore_signal(barrier, inc=1, device_id=axis, device_id_type=MESH)

    loop(1, Z, lambda k: greet(ctx=p.ctx_of(p.z_at(k), y, c)))
    for k in range(1, Y):
        for cc in range(C):
            greet(ctx=p.ctx_of(z, p.y_at(k), cc))
    greet(ctx=p.ctx_of(z, y, 1 - c))
    def greet_tp(k):
        for cc in range(C):
            greet(ctx=p.ctx_of(z, y, cc), tp=p.tp_at(k))

    loop(1, T, greet_tp)
    for copy in [kv_load(s)[i] for i in (1, 0) for s in range(SEQS)]:
        copy.start()
    w_load.start()

    for copy in small:
        copy.wait()
    own = qin[...].astype(F32)
    for s in range(SEQS):
        for hd in range(HEADS):
            qrow[s * HEADS + hd:s * HEADS + hd + 1, :] = own[s:s + 1, hd * HD:(hd + 1) * HD]
    qbuf[y, c, z] = qrow[...].astype(BF16)
    qg = Gather(p, lambda yy: qbuf.at[yy, c], qsems)
    ag = Gather(p, lambda yy: abuf.at[yy], asems)
    pl.semaphore_wait(barrier, (Z - 1) + (Y * C - 1) + (T - 1) * C)
    qg.start()
    nk, nv = nkin[...].astype(F32), nvin[...].astype(F32)
    for s in range(SEQS):
        nkb[s] = jnp.broadcast_to(nk[s:s + 1], (PAD, HD)).astype(BF16)
        nvb[s] = jnp.broadcast_to(nv[s:s + 1], (8, HD))
    for pr in range(SEQS // 2):
        qd[pr] = jnp.zeros((2 * HD, 2 * rows), BF16)
        vt[pr, 2 * HD:, :] = jnp.ones((PAD, kbuf.shape[1]), BF16)

    def transpose(s):
        kv_load(s)[1].wait()
        at = pl.multiple_of(lax.rem(s, 2) * HD, HD)
        vt[s // 2, pl.ds(at, HD), :] = vbuf[s].T

    def attend(k):
        block = p.y_at(-k)
        x = qbuf[block].astype(F32).reshape(slots, SEQS, HEADS, HD)
        for s in range(SEQS):
            j = s % 2
            qd[s // 2, j * HD:(j + 1) * HD, j * rows:(j + 1) * rows] = x[:, s].reshape(rows, HD).T.astype(BF16)
        slot = lax.div(lax.rem(iota((8, 2 * rows), 1), rows), HEADS)
        token = lax.rem(slot, Z) * (Y * C) + block * C + lax.div(slot, Z)
        visible = token >= p.ctx
        chunk = min(CHUNK, kbuf.shape[1])
        chunks = [slice(a, a + chunk) for a in range(0, kbuf.shape[1], chunk)]

        def score(pr, at):
            keys = jnp.concatenate([kbuf[2 * pr, at], kbuf[2 * pr + 1, at]], axis=1)
            raw = jnp.dot(keys, qd[pr], preferred_element_type=F32)
            sbuf[pr, at] = raw
            return jnp.max(raw.reshape(chunk // 8, 8, 2 * rows), axis=0)

        def peak_of(pr, tops):
            keys = jnp.concatenate([nkb[2 * pr], nkb[2 * pr + 1]], axis=1)
            fresh = jnp.dot(keys, qd[pr], preferred_element_type=F32)[:8]
            fresh = jnp.where(visible, fresh, -jnp.inf)
            top = jnp.max(functools.reduce(jnp.maximum, tops + [fresh]), axis=0, keepdims=True)
            peak = rounded(top * SCALE)
            return peak, jnp.exp2(fresh * SCALE - peak)

        def weigh(pr, at, peak):
            pbuf[pr, at] = jnp.exp2(sbuf[pr, at] * SCALE - peak).astype(BF16)

        def finish(pr, peak, fresh):
            out = jnp.dot(vt[pr], pbuf[pr], preferred_element_type=F32)
            sub = iota((8, 2 * rows), 0)
            total = out[2 * HD:2 * HD + 8] + fresh
            three = jnp.where(sub == 0, peak, jnp.where(sub == 1, total, fresh))
            lane = iota((rows, HD), 1)
            row = iota((rows, HD), 0)
            for j in range(2):
                s = 2 * pr + j
                at = slice(j * rows, (j + 1) * rows)
                numer = out[j * HD:(j + 1) * HD, at].T
                cols = three[:, at].T
                numer = numer + rounded(cols[:, 2:3]) * nvb[s][:1]
                lead = rounded(cols[:, 1:2])
                rest = rounded(cols[:, 1:2] - lead)
                head = lax.rem(row, HEADS) + s * HEADS
                entry = jnp.where(lane == head, cols[:, 0:1], jnp.where(lane == head + 64, lead, jnp.where(lane == head + 96, rest, 0.0)))
                packed = jnp.sum(entry.reshape(slots, HEADS, HD), axis=1).reshape(C, Z, HD)
                st[k] = packed if s == 0 else st[k] + packed
                nb[k, :, :, s * HEADS:(s + 1) * HEADS, :] = numer.reshape(C, Z, HEADS, HD)

        tops = [score(0, at) for at in chunks]
        first = peak_of(0, tops)
        tops = []
        for at in chunks:
            tops.append(score(1, at))
            weigh(0, at, first[0])
        second = peak_of(1, tops)
        finish(0, *first)
        for at in chunks:
            weigh(1, at, second[0])
        finish(1, *second)

    def c_copy(k, group, send):
        block = qbuf.at[p.y_at(-k), c if send else 1 - c, qg.rows(group)]
        return p.copy(block, block, csems.at[0, group, k], csems.at[1, group, k], ctx=p.ctx_of(z, y, 1 - c))

    def w_copy():
        return p.copy(wbuf.at[c], wbuf.at[c], wsem.at[0], wsem.at[1], ctx=p.ctx_of(z, y, 1 - c))

    def core_at(j):
        return c if j == 0 else 1 - c

    def y_copy(k, j):
        dev = p.ctx_of(z, p.y_at(-k), core_at(j))
        return p.copy(ysb.at[k, j], yrb.at[k, j], ry.at[0, k, j], ry.at[1, k, j], ctx=dev)

    owners = Z // 2
    mine = z - Z // 4
    owner = (mine >= 0) & (mine < owners)

    def z_copies(o, index):
        dev = p.ctx_of(Z // 4 + o, y, c)
        at = pl.ds(2 * o, 2)
        return (p.copy(zsb.at[at], zrb.at[index], rz.at[0, 0, o], rz.at[1, 0, index], ctx=dev),
                p.copy(zss.at[at], zrs.at[index], rz.at[0, 1, o], rz.at[1, 1, index], ctx=dev))

    def others(last, here, body):
        def one(i):
            @pl.when(i != here)
            def _():
                body(i)
        loop(0, last, one)

    def a_copy(to, o):
        block = abuf.at[y, pl.ds(2 * o, 2)]
        return p.copy(block, block, az.at[0, to], az.at[1, o], ctx=p.ctx_of(to, y, c))

    def t_copy(k, j):
        to = p.tp_at(k)
        return p.copy(ts.at[to * C + core_at(j)], tr.at[k * C + j], tt.at[0], tt.at[1], ctx=p.ctx_of(z, y, core_at(j)), tp=to)

    def t_all():
        block = tr.at[pl.ds(1, T * C - 1)]
        return p.copy(block, block, tt.at[0], tt.at[1], ctx=p.ctx_of(z, y, 1 - c))

    def message(stats, numer):
        pad = jnp.concatenate([stats, jnp.zeros((PAD - Z, HD), F32)], axis=0)
        return jnp.concatenate([numer.reshape(Z * UNIT, HD), pad], axis=0).astype(BF16)

    def reduce_y(k):
        ysb[k, 1] = message(st[k, 1 - c], nb[k, 1 - c])
        y_copy(k, 1).start()

        @pl.when(k > 0)
        def _():
            ysb[k, 0] = message(st[k, c], nb[k, c])
            y_copy(k, 0).start()

    def received(k, j):
        y_copy(k, j).wait_recv()
        got = yrb[k, j].astype(F32)
        return got[Z * UNIT:Z * UNIT + Z], got[:Z * UNIT].reshape(Z, UNIT, HD)

    def reduce_z():
        early = [(st[0, c], nb[0, c]), received(0, 1)] + [received(k, j) for k in units[:-1] for j in range(C)]
        peak, total, numer = merge(*zip(*early))
        late = [(pack(peak, total), numer)] + [received(units[-1], j) for j in range(C)]
        peak, total, numer = merge(*zip(*late))
        stats = pack(peak, total)
        zsb[...] = numer.astype(BF16)
        for k in range(Z):
            zss[k] = stats[k:k + 1]

        def send(o):
            for copy in z_copies(o, z):
                copy.start()
        others(owners, mine, send)

    def attended():
        at = pl.ds(2 * mine, 2)
        zrb[z] = zsb[at]
        zrs[z] = zss[at]

        def wait(i):
            for copy in z_copies(mine, i):
                copy.wait_recv()
        others(Z, z, wait)
        stats = [jnp.concatenate([zrs[i, 0], zrs[i, 1]], axis=0) for i in range(Z)]
        peak, total, numer = merge(stats, [zrb[i].astype(F32) for i in range(Z)])
        abuf[y, at] = (numer / spread(total, 64)).astype(BF16)

        def send(j):
            to = lax.rem(z + Z // 2 + j, Z)

            @pl.when(to != z)
            def _():
                a_copy(to, mine).start()
        loop(0, Z, send)

    def project(group):
        for k in near:
            ag.y_copy(k, group, False).wait_recv()
        H = Z // 2
        n = Y * H * SEQS
        af[...] = abuf[:, ag.rows(group)].reshape(n * HEADS, HD).astype(F32)
        heads = [af[pl.ds(hd, n, stride=HEADS), :].astype(BF16) for hd in range(HEADS)]
        both = jnp.dot(jnp.concatenate(heads, axis=1), jnp.concatenate([wbuf[0], wbuf[1]], axis=1), preferred_element_type=F32)
        for cc in range(C):
            pf[group, cc] = both[:, cc * HD:(cc + 1) * HD]
        for zz in range(H):
            t = ag.half_at(group) * H + zz
            for cc in range(C):
                tile = [pf[group, cc, pl.ds(SEQS * zz + s, Y, stride=SEQS * H), :] for s in range(SEQS)]
                tile = jnp.concatenate(tile, axis=0)
                tf[t * C + cc] = tile
                ts[t * C + cc] = tile.astype(BF16)

        def send(zz):
            k = lax.rem(ag.half_at(group) * H + zz - p.tp + T, T)

            @pl.when(k > 0)
            def _():
                t_copy(k, 0).start()
            t_copy(k, 1).start()
        loop(0, H, send)

    loop(0, SEQS // 2, transpose)
    for group in range(2):
        qg.z_arrived(group)
        c_copy(0, group, True).start()
        qg.along_y(group, units)
    w_load.wait()
    w_copy().start()
    loop(SEQS // 2, SEQS, transpose)
    loop(0, SEQS, lambda s: kv_load(s)[0].wait())

    def unit(i):
        k = unit_at(i)
        for group in range(2):
            c_copy(k, group, False).wait_recv()
        attend(k)
        reduce_y(k)

        @pl.when(i == 0)
        def _():
            for k in near:
                qg.arrived(k)
                for group in range(2):
                    c_copy(k, group, True).start()

    loop(0, Y, unit)
    reduce_z()
    pl.when(owner)(attended)
    w_copy().wait_recv()
    for group in range(2):
        for o in range(owners // 2):
            at = ag.half_at(group) * (owners // 2) + o

            @pl.when(at != mine)
            def _():
                a_copy(z, at).wait_recv()
        ag.along_y(group, units)
    for group in range(2):
        project(group)
    same = tf[p.tp * C + c]
    t_all().wait_recv()
    for k in range(1, T):
        same = same + tr[k * C].astype(F32)
    other = sum(tr[k * C + 1].astype(F32) for k in range(T))
    for s in range(SEQS):
        of[pl.ds(s * Y * C + c, Y, stride=C), :] = same[s * Y:(s + 1) * Y]
        of[pl.ds(s * Y * C + 1 - c, Y, stride=C), :] = other[s * Y:(s + 1) * Y]
    o_ref[...] = of[...].astype(BF16)

    qg.drain(True)
    ag.drain(False)
    w_copy().wait_send()
    for k in range(Y):
        for group in range(2):
            c_copy(k, group, True).wait_send()
        for j in range(C):
            if k + j:
                y_copy(k, j).wait_send()

    def sent(o):
        for copy in z_copies(o, z):
            copy.wait_send()
    others(owners, mine, sent)

    @pl.when(owner)
    def _():
        others(Z, z, lambda to: a_copy(to, mine).wait_send())

    t_all().wait_send()


def build(sizes, queries, keys, values, new_keys, new_values, weight):
    Z, Y, C, T = sizes
    S = keys.shape[1]
    V = pltpu.VMEM
    dma = pltpu.SemaphoreType.DMA
    slots = C * Z
    rows = slots * HEADS
    out_rows = SEQS * Y * C
    block = Z * UNIT + PAD
    tile = SEQS * Y
    scratch = [
        V((SEQS, S, HD), BF16), V((SEQS, S, HD), BF16), V((SEQS // 2, 2 * HD + PAD, S), BF16), V((C,) + weight.shape, BF16),
        V((SEQS, HEADS * HD), BF16), V((SEQS, HD), BF16), V((SEQS, HD), BF16),
        V((SEQS, PAD, HD), BF16), V((SEQS, 8, HD), F32), V((UNIT, HD), F32),
        V((Y, C, Z, UNIT, HD), BF16), V((SEQS // 2, 2 * HD, 2 * rows), BF16),
        V((SEQS // 2, S, 2 * rows), F32), V((SEQS // 2, S, 2 * rows), BF16),
        V((Y, C, Z, UNIT, HD), F32), V((Y, C, Z, HD), F32),
        V((Y, C, block, HD), BF16), V((Y, C, block, HD), BF16),
        V((Z, UNIT, HD), BF16), V((Z, 1, HD), F32),
        V((Z, 2, UNIT, HD), BF16), V((Z, 2, 1, HD), F32),
        V((Y, Z, UNIT, HD), BF16), V((Y * Z // 2 * UNIT, HD), F32), V((2, C, Y * Z // 2 * SEQS, HD), F32),
        V((T * C, tile, HD), F32), V((T * C, tile, HD), BF16), V((T * C, tile, HD), BF16), V((out_rows, HD), F32),
        dma((4 + 2 * SEQS,)), [dma((2, 2)), dma((2, Y - 1)), dma((2, Y - 1))], dma((2, 2, Y)),
        [dma((2, 2)), dma((2, Y - 1)), dma((2, Y - 1))], dma((2,)), dma((2, Y, C)),
        dma((2, 2, Z)), dma((2, Z)), dma((2,)),
    ]
    out = pl.pallas_call(
        functools.partial(kernel, sizes),
        out_shape=jax.ShapeDtypeStruct((out_rows, HD), BF16),
        in_specs=[pl.BlockSpec(memory_space=pltpu.HBM)] * 6,
        out_specs=pl.BlockSpec(memory_space=pltpu.VMEM),
        scratch_shapes=scratch,
        compiler_params=pltpu.CompilerParams(
            collective_id=0, has_side_effects=True, vmem_limit_bytes=64 * 1024 * 1024
        ),
        cost_estimate=pl.CostEstimate(
            flops=4 * SEQS * Y * rows * S * HD, bytes_accessed=4 * SEQS * S * HD,
            transcendentals=SEQS * Y * rows * S,
        ),
    )(
        queries.reshape(SEQS, HEADS * HD), keys, values,
        new_keys.reshape(SEQS, HD), new_values.reshape(SEQS, HD), weight,
    )
    return out.reshape(SEQS, Y * C, HD)


def solution(mesh):
    Z = mesh.shape["tp"]
    sizes = (Z, mesh.shape["ctx"] // (2 * Z), 2, mesh.shape["tp"])
    spec = P(None, "ctx", "tp")
    return jax.shard_map(
        functools.partial(build, sizes),
        mesh=mesh,
        in_specs=(spec, spec, spec, spec, spec, P("tp", "ctx")),
        out_specs=P(None, "tp", "ctx"),
        check_vma=False,
    )
```
